256 devices in a mesh: ctx: 64 (over x, z, core), ch: 4 (over y).
Axes of the slice: x: 4, y: 4, z: 8, core: 2. Of those that a mesh axis runs over, the one named last changes fastest.
Arguments:
- query_proj: bfloat16 [16384, 8192], P('ctx', 'ch'), may hold values from -6 to 6
- key_proj: bfloat16 [16384, 8192], P('ctx', 'ch'), may hold values from -6 to 6
- value_proj: bfloat16 [16384, 8192], P('ctx', 'ch'), may hold values from -6 to 6
- short_filter: float32 [3, 3, 8192], P(None, None, 'ch'), may hold values from -3 to 3
- decay_rate: float32 [16, 8192], P(None, 'ch'), may hold values from 6.1035156e-05 to 0.05
- residue: float32 [16, 8192], P(None, 'ch'), may hold values from -5 to 5
- skip_gain: float32 [8192], P('ch'), may hold values from -4 to 4
- norm_gain: float32 [8192], P('ch'), may hold values from 0.5 to 1.5
- residual: bfloat16 [16384, 8192], P('ctx', 'ch'), may hold values from -6 to 6
- lengths: int32 [4], replicated, may hold values from 1 to 8192, as said below
Outputs:
- stream: float32 [16384, 8192], P('ctx', 'ch')
- normed: float32 [16384, 8192], P('ctx', 'ch')
The draws below stay inside these ranges and needn't reach their ends.
Inputs may be any that keep to these rules, and one draw needn't show every extreme that they name: 4 segment lengths summing to 16384; the second segment is the longest, exactly 8192, and starts after position 2048 and at or before 16384 // 4.
All inputs are finite; a program needn't handle non-finite values.
Results may differ from the reference program's by a relative error of at most 0.0003.
Values may be sent and summed in bfloat16 or wider, within the bound.
No kernel may reach another device: no remote copies, remote signals or barrier semaphores. Data moves between devices by JAX's collectives and lax.ppermute only.
A program may use at most 128 MiB of HBM per device.

```python
import jax
import jax.numpy as jnp
from jax import lax

D = 8192
MODES = 16
TOKENS = 16384


def draw_lengths(key, part):
    key = jax.random.fold_in(key, 11)
    first_key, second_key = jax.random.split(key)
    longest = TOKENS // 2
    first_len = jax.random.randint(first_key, (), TOKENS // 8 + 1, TOKENS // 4 + 1)
    rest = TOKENS - longest - first_len
    third_len = jax.random.randint(second_key, (), 1, rest)
    fourth_len = rest - third_len
    return jnp.stack([first_len, jnp.full((), longest, jnp.int32), third_len, fourth_len]).astype(jnp.int32)


def draw_decay_rate(key, part):
    key = jax.random.fold_in(key, 5)
    pick_key, wide_key, slow_key = jax.random.split(key, 3)
    lowest = jnp.log(jnp.float32(1.0 / TOKENS))
    slow_top = min(16.0 / TOKENS, 0.05)
    wide_rates = jnp.exp(lowest + (jnp.log(jnp.float32(0.05)) - lowest) * jax.random.uniform(wide_key, (MODES, D), jnp.float32))
    slow_rates = jnp.exp(lowest + (jnp.log(jnp.float32(slow_top)) - lowest) * jax.random.uniform(slow_key, (MODES, D), jnp.float32))
    share = 0.34
    chosen = jax.random.uniform(pick_key, (1, D), jnp.float32) < share
    rates = jnp.where(chosen, slow_rates, wide_rates)
    return jnp.clip(rates, 1.0 / TOKENS, 0.05).astype(jnp.float32)


def levels(own_key, shape, cuts, low, high):
    def one(axis_at, blocks):
        draws = jax.random.uniform(jax.random.fold_in(jax.random.fold_in(own_key, 6), axis_at), (blocks,), jnp.float32, low / len(cuts), high / len(cuts))
        return jnp.repeat(jnp.exp(draws), shape[axis_at] // blocks).reshape((-1,) + (1,) * (len(shape) - axis_at - 1))

    factor_of = one(*cuts[0])
    for cut in cuts[1:]:
        factor_of = factor_of * one(*cut)
    return factor_of


def centred(rng, extent, width, most, pieces=(), kind=jnp.bfloat16):
    factor_of = levels(rng, extent, pieces, -0.22, 0.18) if pieces else 1.0
    drawn = jax.random.normal(rng, extent, jnp.float32) * width * factor_of
    return jnp.minimum(jnp.maximum(drawn, -most), most).astype(kind)


def setup_inputs(seed: int = 0) -> dict:
    key_of = jax.random.split(jax.random.key(seed), 11)
    query_proj = centred(key_of[0], (TOKENS, D), 1.0, 6.0, ((0, 64), (1, 4)))
    key_proj = centred(key_of[1], (TOKENS, D), 1.0, 6.0, ((0, 64), (1, 4)))
    value_proj = centred(key_of[2], (TOKENS, D), 1.0, 6.0, ((0, 64), (1, 4)))
    short_filter = centred(key_of[3], (3, 3, D), 0.5, 3.0, ((2, 4),), jnp.float32)
    decay_rate = draw_decay_rate(jax.random.fold_in(key_of[10], 71), 0)
    residue = centred(key_of[5], (MODES, D), 1.0, 5.0, ((1, 4),), jnp.float32)
    skip_gain = centred(key_of[6], (D,), 1.0, 4.0, ((0, 4),), jnp.float32)
    norm_gain = jnp.clip(1.0 + 0.1 * jax.random.normal(key_of[7], (D,), jnp.float32), 0.5, 1.5)
    residual = centred(key_of[8], (TOKENS, D), 1.0, 6.0, ((0, 64), (1, 4)))
    lengths = draw_lengths(jax.random.fold_in(key_of[10], 71), 0)
    return {"query_proj": query_proj, "key_proj": key_proj, "value_proj": value_proj, "short_filter": short_filter, "decay_rate": decay_rate, "residue": residue, "skip_gain": skip_gain, "norm_gain": norm_gain, "residual": residual, "lengths": lengths}


def short_pass(signal, taps, same_one, same_two):
    whole = signal.astype(jnp.float32)
    width_all = whole.shape[1]
    shifted_one = jnp.concatenate([jnp.zeros((1, width_all), jnp.float32), whole[:-1]], axis=0)
    shifted_two = jnp.concatenate([jnp.zeros((2, width_all), jnp.float32), whole[:-2]], axis=0)
    return taps[0] * whole + taps[1] * shifted_one * same_one[:, None] + taps[2] * shifted_two * same_two[:, None]

def reference(query_proj, key_proj, value_proj, short_filter, decay_rate, residue, skip_gain, norm_gain, residual, lengths):
    starts_at = (jnp.cumsum(lengths) - lengths).astype(jnp.int32)
    positions = jnp.arange(TOKENS, dtype=jnp.int32)
    segment_of = (lax.optimization_barrier(jnp.sum((positions[:, None] >= starts_at[None, :]).astype(jnp.int32), axis=1)) - 1).astype(jnp.int32)
    resets = jnp.any(positions[:, None] == starts_at[None, :], axis=1)
    keep_mask = 1.0 - resets.astype(jnp.float32)
    minus_one = jnp.full((1,), -1, jnp.int32)
    minus_two = jnp.full((2,), -1, jnp.int32)
    prev_one = jnp.concatenate([minus_one, segment_of[:-1]]).astype(jnp.int32)
    prev_two = jnp.concatenate([minus_two, segment_of[:-2]]).astype(jnp.int32)
    same_one = (segment_of == prev_one).astype(jnp.float32)
    same_two = (segment_of == prev_two).astype(jnp.float32)
    query_short = short_pass(query_proj, short_filter[0], same_one, same_two)
    key_short = short_pass(key_proj, short_filter[1], same_one, same_two)
    value_short = short_pass(value_proj, short_filter[2], same_one, same_two)
    gated = key_short * value_short
    decay = jnp.exp(-decay_rate)
    pole_gain = residue * jnp.sqrt(-jnp.expm1(-2.0 * decay_rate))

    def advance(state, inputs):
        keep_now, input_now = inputs
        state = keep_now * decay * state + input_now[None, :]
        return (state, lax.optimization_barrier(jnp.sum(pole_gain * state, axis=0)))
    start_state = jnp.zeros(decay_rate.shape, jnp.float32)
    _, long_out = lax.scan(advance, start_state, (keep_mask, gated))
    stream = residual.astype(jnp.float32) + query_short * (long_out + skip_gain * gated)
    power = lax.optimization_barrier(jnp.sum(stream * stream, axis=1))
    scale = lax.rsqrt(power / D + 1e-06)
    normed = stream * scale[:, None] * norm_gain
    return (stream, normed)
```

```python
import functools

import jax
import jax.numpy as jnp
from jax import lax
from jax.experimental import pallas as pl
from jax.experimental.pallas import tpu as pltpu
from jax.sharding import PartitionSpec as P

LANES = 128
CHUNKS = 8
GROUP = 512
STEPS = 8
F32 = jnp.float32
BF16 = jnp.bfloat16


def starts_of(lengths_ref):
    first = lengths_ref[0]
    second = first + lengths_ref[1]
    third = second + lengths_ref[2]
    return (first, second, third)


def spread(row):
    return jnp.broadcast_to(row, (CHUNKS, LANES))


def no_start(starts, where):
    kept = jnp.ones(where.shape, jnp.bool_)
    for start in starts:
        kept = kept & (where != start)
    return kept.astype(F32)


def any_in(starts, low, high):
    found = jnp.bool_(False)
    for start in starts:
        found = found | ((start >= low) & (start < high))
    return found


def block_has_start(starts, base, rows, block):
    found = jnp.bool_(False)
    for start in starts:
        inside = start - base
        place = lax.rem(jnp.maximum(inside, 0), rows // CHUNKS)
        found = found | (
            (inside >= 0) & (inside < rows) & (place >= block * STEPS) & (place < (block + 1) * STEPS)
        )
    return found


def lanes_at(part):
    return pl.ds(pl.multiple_of(part * LANES, LANES), LANES)


def chunk_of(place):
    return pl.ds(pl.multiple_of(place * CHUNKS, CHUNKS), CHUNKS)


def lay_out(source, lanes, target, span, offset):
    for piece in range(CHUNKS):
        low = offset + piece * (span + 1)
        target[low : low + span, :] = source[piece * span : (piece + 1) * span, lanes].astype(F32)


def column_copies(sources, targets, sems, group):
    lanes = pl.ds(pl.multiple_of(group * GROUP, GROUP), GROUP)
    return [
        pltpu.make_async_copy(source.at[:, lanes], target.at[:, lanes], sems.at[i, group])
        for i, (source, target) in enumerate(zip(sources, targets))
    ]


def rim_kernel(q_hbm, k_hbm, v_hbm, out_ref, buffer, sems):
    tail = buffer.shape[1]
    copies = [
        pltpu.make_async_copy(source.at[pl.ds(source.shape[0] - tail, tail), :], buffer.at[i], sems.at[i])
        for i, source in enumerate((q_hbm, k_hbm, v_hbm))
    ]
    for copy in copies:
        copy.start()
    for i, copy in enumerate(copies):
        copy.wait()
        out_ref[i] = buffer[i, tail - 2 :, :]


def walk(span, starts, base, rows, run, carry):
    def one_block(block, carry):
        flag = block_has_start(starts, base, rows, block)
        return lax.cond(
            flag, functools.partial(run, block, True), functools.partial(run, block, False), carry
        )

    return lax.fori_loop(0, span // STEPS, one_block, carry)


def end_kernel(rows, poles, lengths_ref, k_hbm, v_hbm, rim_ref, taps_hbm, rate_hbm, gated_a, gated_hbm, local_hbm, end_ref, rim_hbm, k_ref, v_ref, gated_b, local_ref, taps_ref, rate_ref, kx, vx, decay_ref, sems, out_sems, local_sems, small_sems):
    span = rows // CHUNKS
    starts = starts_of(lengths_ref)
    base = lax.axis_index("ctx") * rows
    chunk = lax.broadcasted_iota(jnp.int32, (CHUNKS, LANES), 0)
    chunk_row = base + chunk * span
    small = [
        pltpu.make_async_copy(taps_hbm, taps_ref, small_sems.at[0]),
        pltpu.make_async_copy(rate_hbm, rate_ref, small_sems.at[1]),
    ]
    pass_on = pltpu.make_async_copy(rim_ref.at[0], rim_hbm, small_sems.at[2])
    groups = k_ref.shape[1] // GROUP
    for group in range(groups):
        for copy in column_copies((k_hbm, v_hbm), (k_ref, v_ref), sems, group):
            copy.start()
        if group == 0:
            for copy in small:
                copy.start()
    pass_on.start()
    for copy in small:
        copy.wait()
    far = no_start(starts, chunk_row - 1)
    alive = jnp.ones((CHUNKS, LANES), jnp.bool_)
    for start in starts:
        alive = alive & ((start < chunk_row) | (start >= chunk_row + span))
    joined = (alive & (chunk > 0)).astype(F32)

    inner = GROUP // LANES

    def store(here):
        return pltpu.make_async_copy(gated_b.at[here], gated_hbm.at[here], out_sems.at[here])

    def store_local(part):
        return pltpu.make_async_copy(local_ref.at[part], local_hbm.at[part], local_sems.at[part])

    def one_group(group, first, gated_ref):
        for copy in column_copies((k_hbm, v_hbm), (k_ref, v_ref), sems, group):
            copy.wait()

        @pl.loop(group * inner, (group + 1) * inner)
        def _(part):
            lanes = lanes_at(part)
            here = part - first * inner
            for i, source, target in ((1, k_ref, kx), (2, v_ref, vx)):
                target[5:7, :] = rim_ref[i, :, lanes].astype(F32)
                lay_out(source, lanes, target, span, 8)
            decay_ref[...] = jnp.exp(-rate_ref[:, lanes])
            taps = [[spread(taps_ref[i, j : j + 1, lanes]) for j in range(3)] for i in (1, 2)]
            decay = [spread(decay_ref[m : m + 1, :]) for m in range(poles)]
            carry = (
                kx[pl.ds(6, CHUNKS, stride=span + 1), :],
                kx[pl.ds(5, CHUNKS, stride=span + 1), :] * far,
                vx[pl.ds(6, CHUNKS, stride=span + 1), :],
                vx[pl.ds(5, CHUNKS, stride=span + 1), :] * far,
            ) + tuple(jnp.zeros((CHUNKS, LANES), F32) for _ in range(poles))

            def run(block, masked, carry):
                carry = list(carry)
                for step in range(STEPS):
                    place = block * STEPS + step
                    if masked:
                        keep = no_start(starts, chunk_row + place)
                        carry = [held * keep for held in carry]
                    row = pl.ds(8 + place, CHUNKS, stride=span + 1)
                    key = kx[row, :]
                    value = vx[row, :]
                    key_short = taps[0][0] * key + taps[0][1] * carry[0] + taps[0][2] * carry[1]
                    value_short = taps[1][0] * value + taps[1][1] * carry[2] + taps[1][2] * carry[3]
                    gated = key_short * value_short
                    gated_ref[here, chunk_of(place), :] = gated
                    states = [decay[m] * carry[4 + m] + gated for m in range(poles)]
                    carry = [key, carry[0], value, carry[2]] + states
                return tuple(carry)

            carry = walk(span, starts, base, rows, run, carry)
            for m in range(poles):
                rate = spread(rate_ref[m : m + 1, lanes])
                reach = jnp.exp(-float(span) * rate) * joined
                state = carry[4 + m]
                for hop in (1, 2, 4):
                    state = state + reach * pltpu.roll(state, hop, 0)
                    if hop < 4:
                        reach = reach * pltpu.roll(reach, hop, 0)
                end_ref[part, m : m + 1, :] = state[CHUNKS - 1 :, :]
                local_ref[part, m * CHUNKS : (m + 1) * CHUNKS, :] = jnp.where(
                    chunk > 0, pltpu.roll(state, 1, 0), 0.0
                )
            store_local(part).start()
            if first:
                store(here).start()

    middle = gated_a.shape[0] // inner
    pl.loop(0, middle)(lambda group: one_group(group, 0, gated_a))
    pl.loop(middle, groups)(lambda group: one_group(group, middle, gated_b))
    pass_on.wait()
    for here in range(gated_b.shape[0]):
        store(here).wait()
    for part in range(local_ref.shape[0]):
        store_local(part).wait()


def scan_kernel(rows, poles, lengths_ref, rate_ref, pieces_ref, out_ref):
    starts = starts_of(lengths_ref)
    ranks, held = pieces_ref.shape[:2]
    shares = poles // held
    mine = lax.axis_index("ctx")
    lanes = lanes_at(lax.div(mine, shares))
    rate = rate_ref[:held, lanes]
    for share in range(1, shares):
        theirs = rate_ref[share * held : (share + 1) * held, lanes]
        rate = jnp.where(lax.rem(mine, shares) == share, theirs, rate)
    whole = jnp.exp(-float(rows) * rate)
    running = jnp.zeros((held, LANES), F32)
    for rank in range(ranks):
        out_ref[rank] = running
        alive = jnp.where(any_in(starts, rank * rows, (rank + 1) * rows), 0.0, 1.0)
        running = (alive * whole) * running + pieces_ref[rank]


def near_kernel(rows, poles, first, lengths_ref, q_hbm, res_hbm, rim_hbm, taps_hbm, rate_hbm, gain_ref, skip_ref, gated_in, local_hbm, near_ref, query_out, q_ref, r_ref, local_ref, rim_ref, taps_ref, rate_ref, qx, rx, decay_ref, sems, local_sems, small_sems, *moved):
    span = rows // CHUNKS
    starts = starts_of(lengths_ref)
    base = lax.axis_index("ctx") * rows
    chunk = lax.broadcasted_iota(jnp.int32, (CHUNKS, LANES), 0)
    chunk_row = base + chunk * span
    small = [
        pltpu.make_async_copy(taps_hbm, taps_ref, small_sems.at[0]),
        pltpu.make_async_copy(rate_hbm, rate_ref, small_sems.at[1]),
        pltpu.make_async_copy(rim_hbm, rim_ref, small_sems.at[2]),
    ]
    for copy in small:
        copy.start()
    inner = GROUP // LANES
    gated_ref, query_ref, gated_sems, query_sems = moved or (gated_in, query_out, None, None)

    def fetch_local(here):
        source = local_hbm.at[here + first * inner]
        return pltpu.make_async_copy(source, local_ref.at[here], local_sems.at[here])

    def fetch(here):
        return pltpu.make_async_copy(gated_in.at[here], gated_ref.at[here], gated_sems.at[here])

    def store(here):
        return pltpu.make_async_copy(query_ref.at[here], query_out.at[here], query_sems.at[here])

    count = near_ref.shape[0] // inner
    for group in range(first, first + count):
        for copy in column_copies((q_hbm, res_hbm), (q_ref, r_ref), sems, group):
            copy.start()
        for here in range((group - first) * inner, (group - first + 1) * inner):
            fetch_local(here).start()
            if moved:
                fetch(here).start()
    for copy in small:
        copy.wait()
    far = no_start(starts, chunk_row - 1)

    @pl.loop(first, first + count)
    def _(group):
        for copy in column_copies((q_hbm, res_hbm), (q_ref, r_ref), sems, group):
            copy.wait()

        @pl.loop(group * inner, (group + 1) * inner)
        def _(part):
            lanes = lanes_at(part)
            here = part - first * inner
            fetch_local(here).wait()
            if moved:
                fetch(here).wait()
            qx[5:7, :] = rim_ref[:, lanes].astype(F32)
            lay_out(q_ref, lanes, qx, span, 8)
            lay_out(r_ref, lanes, rx, span, 0)
            decay_ref[...] = jnp.exp(-rate_ref[:, lanes])
            taps = [spread(taps_ref[0, j : j + 1, lanes]) for j in range(3)]
            skip = spread(skip_ref[:, lanes])
            decay = [spread(decay_ref[m : m + 1, :]) for m in range(poles)]
            gain = [spread(gain_ref[m : m + 1, lanes]) for m in range(poles)]
            carry = [
                qx[pl.ds(6, CHUNKS, stride=span + 1), :],
                qx[pl.ds(5, CHUNKS, stride=span + 1), :] * far,
            ] + [local_ref[here, m * CHUNKS : (m + 1) * CHUNKS, :] for m in range(poles)]

            def run(block, masked, carry):
                carry = list(carry)
                for step in range(STEPS):
                    place = block * STEPS + step
                    if masked:
                        keep = no_start(starts, chunk_row + place)
                        carry = [held * keep for held in carry]
                    query = qx[pl.ds(8 + place, CHUNKS, stride=span + 1), :]
                    query_short = taps[0] * query + taps[1] * carry[0] + taps[2] * carry[1]
                    gated = gated_ref[here, chunk_of(place), :]
                    states = [decay[m] * carry[2 + m] + gated for m in range(poles)]
                    total = skip * gated
                    for m in range(poles):
                        total = total + gain[m] * states[m]
                    query_ref[here, chunk_of(place), :] = query_short
                    near_ref[here, chunk_of(place), :] = (
                        rx[pl.ds(place, CHUNKS, stride=span + 1), :] + query_short * total
                    )
                    carry = [query, carry[0]] + states
                return tuple(carry)

            walk(span, starts, base, rows, run, tuple(carry))
            if moved:
                store(here).start()

    if moved:
        for here in range(near_ref.shape[0]):
            store(here).wait()


def stream_kernel(rows, poles, lengths_ref, rate_ref, gain_ref, incoming_ref, near_a, query_a, near_b, query_hbm, out_hbm, stream_ref, power_ref, query_b, sx, px, decay_ref, sems, query_sems):
    span = rows // CHUNKS
    starts = starts_of(lengths_ref)
    base = lax.axis_index("ctx") * rows
    chunk = lax.broadcasted_iota(jnp.int32, (CHUNKS, LANES), 0)
    chunk_row = base + chunk * span
    ahead = base + rows
    for start in starts:
        ahead = jnp.where((start >= base) & (start < ahead), start, ahead)
    px[...] = jnp.zeros_like(px)
    half = near_a.shape[0]
    inner = GROUP // LANES

    def fetch(here):
        return pltpu.make_async_copy(query_hbm.at[here], query_b.at[here], query_sems.at[here])

    for here in range(half):
        fetch(here).start()
    before = (chunk * span).astype(F32)

    def copy_out(group):
        lanes = pl.ds(pl.multiple_of(group * GROUP, GROUP), GROUP)
        return pltpu.make_async_copy(stream_ref.at[:, lanes], out_hbm.at[:, lanes], sems.at[group])

    def one_part(part, near_ref, query_ref, place_of):
        lanes = lanes_at(part)
        decay_ref[...] = jnp.exp(-rate_ref[:, lanes])
        decay = [spread(decay_ref[m : m + 1, :]) for m in range(poles)]
        carry = []
        for m in range(poles):
            entering = incoming_ref[part, m : m + 1, :] * gain_ref[m : m + 1, lanes]
            carry.append(jnp.exp(-before * spread(rate_ref[m : m + 1, lanes])) * spread(entering))
        for place in range(span):
            carry = [decay[m] * carry[m] for m in range(poles)]
            terms = list(carry)
            while len(terms) > 1:
                terms = [
                    terms[i] + terms[i + 1] if i + 1 < len(terms) else terms[i]
                    for i in range(0, len(terms), 2)
                ]
            carried = jnp.where(chunk_row + place < ahead, terms[0], 0.0)
            here = chunk_of(place)
            sx[pl.ds(place, CHUNKS, stride=span + 1), :] = (
                near_ref[place_of, here, :] + query_ref[place_of, here, :] * carried
            )
        for piece in range(CHUNKS):
            low = piece * (span + 1)
            stream = sx[low : low + span, :]
            native = slice(piece * span, (piece + 1) * span)
            stream_ref[native, lanes] = stream
            px[native, :] += stream * stream

    groups = stream_ref.shape[1] // GROUP
    for side, (near_ref, query_ref) in enumerate(((near_a, query_a), (near_b, query_b))):

        @pl.loop(0, half // inner)
        def _(group):
            @pl.loop(group * inner, (group + 1) * inner)
            def _(part):
                if side:
                    fetch(part).wait()
                one_part(part + side * half, near_ref, query_ref, part)

            copy_out(group + side * (half // inner)).start()

    for piece in range(rows // LANES):
        turned = px[piece * LANES : (piece + 1) * LANES, :].T
        power_ref[piece : piece + 1, :] = jnp.sum(turned, axis=0, keepdims=True)
    for group in range(groups):
        copy_out(group).wait()


def norm_kernel(width, power_ref, gain_ref, stream_ref, out_hbm, scale_ref, buffer, sems):
    scale = lax.rsqrt(jnp.sum(power_ref[...], axis=0) / width + 1e-06)
    for piece in range(scale.shape[0]):
        wide = jnp.broadcast_to(scale[piece : piece + 1, :], (LANES, LANES))
        scale_ref[piece * LANES : (piece + 1) * LANES, :] = wide.T
    rows = stream_ref.shape[0]
    count = sems.shape[0]
    tall = rows // count

    def copy_out(group):
        here = pl.ds(pl.multiple_of(group * tall, tall), tall)
        return pltpu.make_async_copy(buffer.at[here, :], out_hbm.at[here, :], sems.at[group])

    @pl.loop(0, count)
    def _(group):
        here = pl.ds(pl.multiple_of(group * tall, tall), tall)
        factor = scale_ref[here, :]
        for part in range(stream_ref.shape[1] // LANES):
            lanes = slice(part * LANES, (part + 1) * LANES)
            buffer[here, lanes] = stream_ref[here, lanes] * factor * gain_ref[:, lanes]
        copy_out(group).start()

    for group in range(count):
        copy_out(group).wait()


def shifted(block, axis, distance, wrap):
    count = lax.axis_size(axis)
    route = [(i, (i + distance) % count) for i in range(count) if wrap or i + distance < count]
    return lax.ppermute(block, axis, route)


def on_device(query_proj, key_proj, value_proj, short_filter, decay_rate, residue, skip_gain, norm_gain, residual, lengths):
    rows, width = query_proj.shape
    poles = decay_rate.shape[0]
    ranks = lax.axis_size("ctx")
    parts = width // LANES
    span = rows // CHUNKS
    groups = width // GROUP
    numbers = pl.BlockSpec(memory_space=pltpu.SMEM)
    near_by = pl.BlockSpec(memory_space=pltpu.VMEM)
    outside = pl.BlockSpec(memory_space=pltpu.HBM)
    limit = pltpu.CompilerParams(vmem_limit_bytes=12 * 1024 * 1024)
    shape = lambda *dims: jax.ShapeDtypeStruct(dims, F32)
    kept_near = lambda *dims: pltpu.VMEM(dims, F32)
    far_off = lambda array: pltpu.with_memory_space_constraint(array, pltpu.HBM)
    close_by = lambda array: pltpu.with_memory_space_constraint(array, pltpu.VMEM)
    query_proj, key_proj, value_proj, residual, short_filter = map(
        far_off, (query_proj, key_proj, value_proj, residual, short_filter)
    )

    rims = pl.pallas_call(
        rim_kernel,
        in_specs=[outside] * 3,
        out_specs=near_by,
        out_shape=jax.ShapeDtypeStruct((3, 2, width), query_proj.dtype),
        scratch_shapes=[pltpu.VMEM((3, 16, width), BF16), pltpu.SemaphoreType.DMA((3,))],
        name="rims",
    )(query_proj, key_proj, value_proj)
    rims = shifted(rims, "ctx", 1, False)
    pole_gain = residue * jnp.sqrt(-jnp.expm1(-2.0 * decay_rate))
    skip = skip_gain.reshape(1, width)

    half = parts // 2
    gated_a, gated_b, local, end, query_rim = pl.pallas_call(
        functools.partial(end_kernel, rows, poles),
        in_specs=[numbers, outside, outside, near_by, outside, outside],
        out_specs=[near_by, outside, outside, near_by, outside],
        out_shape=[
            kept_near(half, rows, LANES),
            pltpu.HBM((half, rows, LANES), F32),
            pltpu.HBM((parts, poles * CHUNKS, LANES), F32),
            shape(parts, poles, LANES),
            pltpu.HBM((2, width), BF16),
        ],
        scratch_shapes=[
            pltpu.VMEM((rows, width), BF16),
            pltpu.VMEM((rows, width), BF16),
            pltpu.VMEM((half, rows, LANES), F32),
            pltpu.VMEM((parts, poles * CHUNKS, LANES), F32),
            pltpu.VMEM((3, 3, width), F32),
            pltpu.VMEM((poles, width), F32),
            pltpu.VMEM((rows + 16, LANES), F32),
            pltpu.VMEM((rows + 16, LANES), F32),
            pltpu.VMEM((poles, LANES), F32),
            pltpu.SemaphoreType.DMA((2, groups)),
            pltpu.SemaphoreType.DMA((half,)),
            pltpu.SemaphoreType.DMA((parts,)),
            pltpu.SemaphoreType.DMA((3,)),
        ],
        compiler_params=limit,
        name="end_state",
    )(lengths, key_proj, value_proj, rims, short_filter, decay_rate)

    held = parts * poles // ranks
    pieces = lax.all_to_all(end.reshape(ranks, held, LANES), "ctx", 0, 0, tiled=True)

    def near_side(first, count, gated, moved):
        block = (count * (GROUP // LANES), rows, LANES)
        return pl.pallas_call(
            functools.partial(near_kernel, rows, poles, first),
            in_specs=[numbers] + [outside] * 5 + [near_by, near_by, outside if moved else near_by, outside],
            out_specs=[near_by, outside if moved else near_by],
            out_shape=[kept_near(*block), pltpu.HBM(block, F32) if moved else kept_near(*block)],
            scratch_shapes=[
                pltpu.VMEM((rows, width), BF16),
                pltpu.VMEM((rows, width), BF16),
                pltpu.VMEM((block[0], poles * CHUNKS, LANES), F32),
                pltpu.VMEM((2, width), BF16),
                pltpu.VMEM((3, 3, width), F32),
                pltpu.VMEM((poles, width), F32),
                pltpu.VMEM((rows + 16, LANES), F32),
                pltpu.VMEM((rows + 16, LANES), F32),
                pltpu.VMEM((poles, LANES), F32),
                pltpu.SemaphoreType.DMA((2, groups)),
                pltpu.SemaphoreType.DMA((block[0],)),
                pltpu.SemaphoreType.DMA((3,)),
            ]
            + (
                [
                    pltpu.VMEM(block, F32),
                    pltpu.VMEM(block, F32),
                    pltpu.SemaphoreType.DMA((block[0],)),
                    pltpu.SemaphoreType.DMA((block[0],)),
                ]
                if moved
                else []
            ),
            compiler_params=limit,
            cost_estimate=pl.CostEstimate(flops=4000000, bytes_accessed=8000000, transcendentals=0),
            name="near",
        )(
            lengths,
            query_proj,
            residual,
            far_off(query_rim),
            short_filter,
            decay_rate,
            pole_gain,
            skip,
            far_off(gated) if moved else close_by(gated),
            far_off(local),
        )

    near_a, query_a = near_side(0, groups // 2, gated_a, False)
    near_b, query_b = near_side(groups // 2, groups - groups // 2, gated_b, True)
    pieces, near_a = lax.optimization_barrier((pieces, near_a))
    scanned = pl.pallas_call(
        functools.partial(scan_kernel, rows, poles),
        in_specs=[numbers, near_by, near_by],
        out_specs=near_by,
        out_shape=pltpu.HBM((ranks, held, LANES), F32),
        compiler_params=limit,
        name="rank_scan",
    )(lengths, decay_rate, pieces)
    incoming = lax.all_to_all(scanned, "ctx", 0, 0, tiled=True).reshape(parts, poles, LANES)

    stream, kept, power = pl.pallas_call(
        functools.partial(stream_kernel, rows, poles),
        in_specs=[numbers] + [near_by] * 6 + [outside],
        out_specs=[outside, near_by, near_by],
        out_shape=[pltpu.HBM((rows, width), F32), kept_near(rows, width), kept_near(rows // LANES, LANES)],
        scratch_shapes=[
            pltpu.VMEM((half, rows, LANES), F32),
            pltpu.VMEM((rows + 8, LANES), F32),
            pltpu.VMEM((rows, LANES), F32),
            pltpu.VMEM((poles, LANES), F32),
            pltpu.SemaphoreType.DMA((groups,)),
            pltpu.SemaphoreType.DMA((half,)),
        ],
        compiler_params=limit,
        name="stream",
    )(lengths, decay_rate, pole_gain, incoming, *map(close_by, (near_a, query_a, near_b)), far_off(query_b))
    shares = lax.axis_size("ch")
    powers = jnp.stack([power] + [shifted(power, "ch", i, True) for i in range(1, shares)])
    normed = pl.pallas_call(
        functools.partial(norm_kernel, float(width * shares)),
        in_specs=[near_by, near_by, near_by],
        out_specs=outside,
        out_shape=shape(rows, width),
        scratch_shapes=[
            pltpu.VMEM((rows, LANES), F32),
            pltpu.VMEM((rows, width), F32),
            pltpu.SemaphoreType.DMA((8,)),
        ],
        compiler_params=limit,
        name="norm",
    )(powers, norm_gain.reshape(1, width), close_by(kept))
    return (stream, normed)


def solution(mesh):
    placed = (
        P("ctx", "ch"),
        P("ctx", "ch"),
        P("ctx", "ch"),
        P(None, None, "ch"),
        P(None, "ch"),
        P(None, "ch"),
        P("ch"),
        P("ch"),
        P("ctx", "ch"),
        P(),
    )
    return jax.shard_map(
        on_device,
        mesh=mesh,
        in_specs=placed,
        out_specs=(P("ctx", "ch"), P("ctx", "ch")),
        check_vma=False,
    )
```

```python
import functools

import jax
import jax.numpy as jnp
from jax import lax
from jax.experimental import pallas as pl
from jax.experimental.pallas import tpu as pltpu
from jax.sharding import PartitionSpec as P

LANES = 128
CHUNKS = 8
GROUP = 256
FIRST_SHARE = 4
HEAD = 2
READY = 6
STEPS = 16
F32 = jnp.float32
BF16 = jnp.bfloat16


def starts_of(lengths_ref):
    first = lengths_ref[0]
    second = first + lengths_ref[1]
    third = second + lengths_ref[2]
    return (first, second, third)


def spread(row):
    return jnp.broadcast_to(row, (CHUNKS, LANES))


def no_start(starts, where):
    kept = jnp.ones(where.shape, jnp.bool_)
    for start in starts:
        kept = kept & (where != start)
    return kept.astype(F32)


def any_in(starts, low, high):
    found = jnp.bool_(False)
    for start in starts:
        found = found | ((start >= low) & (start < high))
    return found


def block_has_start(starts, base, rows, block):
    found = jnp.bool_(False)
    for start in starts:
        inside = start - base
        place = lax.rem(jnp.maximum(inside, 0), rows // CHUNKS)
        found = found | (
            (inside >= 0) & (inside < rows) & (place >= block * STEPS) & (place < (block + 1) * STEPS)
        )
    return found


def lanes_at(part):
    return pl.ds(pl.multiple_of(part * LANES, LANES), LANES)


def chunk_of(place):
    return pl.ds(pl.multiple_of(place * CHUNKS, CHUNKS), CHUNKS)


def lay_out(source, lanes, target, span, offset):
    for piece in range(CHUNKS):
        low = offset + piece * (span + 1)
        target[low : low + span, :] = source[piece * span : (piece + 1) * span, lanes].astype(F32)


def column_copies(sources, targets, sems, group):
    lanes = pl.ds(pl.multiple_of(group * GROUP, GROUP), GROUP)
    return [
        pltpu.make_async_copy(source.at[:, lanes], target.at[:, lanes], sems.at[i, group])
        for i, (source, target) in enumerate(zip(sources, targets))
    ]


def rim_kernel(q_hbm, k_hbm, v_hbm, out_ref, buffer, sems):
    tail = buffer.shape[1]
    copies = [
        pltpu.make_async_copy(source.at[pl.ds(source.shape[0] - tail, tail), :], buffer.at[i], sems.at[i])
        for i, source in enumerate((q_hbm, k_hbm, v_hbm))
    ]
    for copy in copies:
        copy.start()
    for i, copy in enumerate(copies):
        copy.wait()
        out_ref[i] = buffer[i, tail - 2 :, :]


def walk(span, flags, run, carry):
    for block in range(span // STEPS):
        carry = lax.cond(
            flags[block], functools.partial(run, block, True), functools.partial(run, block, False), carry
        )
    return carry


FAR, JOINED, REACHED, AHEAD, FLAGS, BEGUN, INSIDE = (slice(i * CHUNKS, (i + 1) * CHUNKS) for i in (0, 1, 2, 3, 4, 5, 8))
SECTIONS = 11 * CHUNKS


def describe(starts, base, rows, info_ref):
    span = rows // CHUNKS
    chunk = lax.broadcasted_iota(jnp.int32, (CHUNKS, LANES), 0)
    chunk_row = base + chunk * span
    alive = jnp.ones((CHUNKS, LANES), jnp.bool_)
    reached = jnp.ones((CHUNKS, LANES), jnp.bool_)
    ahead = jnp.full((CHUNKS, LANES), span, jnp.int32)
    for start in starts:
        inside = start - chunk_row
        alive = alive & ((inside < 0) | (inside >= span))
        reached = reached & ((start < base) | (inside >= 0))
        ahead = jnp.where((inside >= 0) & (inside < ahead), inside, ahead)
    info_ref[FAR, :] = no_start(starts, chunk_row - 1)
    info_ref[JOINED, :] = (alive & (chunk > 0)).astype(F32)
    info_ref[REACHED, :] = reached.astype(F32)
    info_ref[AHEAD, :] = ahead.astype(F32)
    for block in range(span // STEPS):
        flag = jnp.where(block_has_start(starts, base, rows, block), 1.0, 0.0)
        info_ref[FLAGS.start + block : FLAGS.start + block + 1, :] = jnp.full((1, LANES), flag, F32)
    for i, start in enumerate(starts):
        rank = lax.div(start, rows).astype(F32)
        low = BEGUN.start + i * CHUNKS
        info_ref[low : low + CHUNKS, :] = jnp.full((CHUNKS, LANES), rank, F32)
        low = INSIDE.start + i * CHUNKS
        info_ref[low : low + CHUNKS, :] = (start - chunk_row).astype(F32)


def pitched(row, span):
    return row + lax.div(row, span)


def end_kernel(rows, poles, lengths_hbm, k_hbm, v_hbm, q_hbm, res_hbm, rim_ref, taps_hbm, rate_hbm, gated_a, gated_hbm, end_hbm, q_next, r_next, rim_next, taps_next, info_ref, lengths_ref, k_ref, v_ref, gated_b, end_ref, taps_ref, rate_ref, kx, vx, gx, decay_ref, sems, out_sems, end_sems, small_sems):
    span = rows // CHUNKS
    base = lax.axis_index("ctx") * rows
    phase = lax.broadcasted_iota(jnp.int32, (CHUNKS, LANES), 0)
    small = [
        pltpu.make_async_copy(source, target, small_sems.at[i])
        for i, (source, target) in enumerate(((lengths_hbm, lengths_ref), (taps_hbm, taps_ref), (rate_hbm, rate_ref)))
    ]
    columns = pl.ds(0, q_next.shape[1])
    ahead_of_time = [
        pltpu.make_async_copy(source.at[:, columns], target, small_sems.at[len(small) + i])
        for i, (source, target) in enumerate(((q_hbm, q_next), (res_hbm, r_next)))
    ]
    groups = k_ref.shape[1] // GROUP
    for copy in small:
        copy.start()
    for group in range(groups):
        for copy in column_copies((k_hbm, v_hbm), (k_ref, v_ref), sems, group):
            copy.start()
    for copy in ahead_of_time:
        copy.start()
    rim_next[...] = rim_ref[0]
    for copy in small:
        copy.wait()
    taps_next[...] = taps_ref[0]
    starts = starts_of(lengths_ref)
    touched = any_in(starts, base - 1, base + rows)
    last = jnp.int32(0)
    for start in starts:
        last = jnp.where((start >= base) & (start < base + rows), start - base, last)
    describe(starts, base, rows, info_ref)
    inner = GROUP // LANES

    def store(here):
        return pltpu.make_async_copy(gated_b.at[here], gated_hbm.at[here], out_sems.at[here])

    def send(group):
        here = pl.ds(group * inner, inner)
        return pltpu.make_async_copy(end_ref.at[here], end_hbm.at[here], end_sems.at[group])

    def one_group(group, first, gated_ref):
        for copy in column_copies((k_hbm, v_hbm), (k_ref, v_ref), sems, group):
            copy.wait()

        @pl.loop(group * inner, (group + 1) * inner)
        def _(part):
            lanes = lanes_at(part)
            here = part - first * inner
            for i, source, target in ((1, k_ref, kx), (2, v_ref, vx)):
                target[6:8, :] = rim_ref[i, :, lanes].astype(F32)
                target[8:, :] = source[:, lanes].astype(F32)
            decay_ref[...] = jnp.exp(-float(CHUNKS) * rate_ref[:, lanes])
            lines = [[taps_ref[i, j : j + 1, lanes] for j in range(3)] for i in (1, 2)]
            taps = [[spread(line) for line in three] for three in lines]
            for block in range(rows // CHUNKS):
                low = block * CHUNKS
                shorts = []
                for three, source in zip(taps, (kx, vx)):
                    short = three[0] * source[low + 8 : low + 16, :]
                    for back in (1, 2):
                        short = short + three[back] * source[low + 8 - back : low + 16 - back, :]
                    shorts.append(short)
                gated = shorts[0] * shorts[1]
                gx[low : low + CHUNKS, :] = gated
                to = low + low // span
                gated_ref[here, to : to + CHUNKS, :] = gated

            @pl.when(touched)
            def _():
                for start in starts:
                    inside = start - base

                    def mend(row, reach):
                        shorts = []
                        for three, source in zip(lines, (kx, vx)):
                            short = three[0] * source[pl.ds(row + 8, 1), :]
                            if reach:
                                short = short + three[1] * source[pl.ds(row + 7, 1), :]
                            shorts.append(short)
                        gated = shorts[0] * shorts[1]
                        gx[pl.ds(row, 1), :] = gated
                        gated_ref[here, pl.ds(pitched(row, span), 1), :] = gated

                    @pl.when((inside >= 0) & (inside < rows))
                    def _():
                        mend(inside, False)

                    @pl.when((inside >= -1) & (inside < rows - 1))
                    def _():
                        mend(inside + 1, True)

                for block in range(rows // CHUNKS):
                    low = block * CHUNKS
                    gx[low : low + CHUNKS, :] = jnp.where(
                        phase + low >= last, gx[low : low + CHUNKS, :], 0.0
                    )

            decay = [spread(decay_ref[m : m + 1, :]) for m in range(poles)]
            sums = [gx[:CHUNKS, :] for _ in range(poles)]
            for block in range(1, rows // CHUNKS):
                gated = gx[block * CHUNKS : (block + 1) * CHUNKS, :]
                sums = [decay[m] * sums[m] + gated for m in range(poles)]
            after = (phase - (CHUNKS - 1)).astype(F32)
            for m in range(poles):
                weight = jnp.exp(after * spread(rate_ref[m : m + 1, lanes]))
                end_ref[part, m : m + 1, :] = jnp.sum(weight * sums[m], axis=0, keepdims=True)
            if first:
                store(here).start()

        send(group).start()

    middle = gated_a.shape[0] // inner
    pl.loop(0, middle)(lambda group: one_group(group, 0, gated_a))
    pl.loop(middle, groups)(lambda group: one_group(group, middle, gated_b))
    for copy in ahead_of_time:
        copy.wait()
    for here in range(gated_b.shape[0]):
        store(here).wait()
    for group in range(groups):
        send(group).wait()


def rank_factors(info_ref, rows, poles, rate_ref, out_ref):
    ranks, held = out_ref.shape[:2]
    shares = poles // held
    mine = lax.axis_index("ctx")
    lanes = lanes_at(lax.div(mine, shares))
    rate = rate_ref[:held, lanes]
    for share in range(1, shares):
        theirs = rate_ref[share * held : (share + 1) * held, lanes]
        rate = jnp.where(lax.rem(mine, shares) == share, theirs, rate)
    whole = jnp.exp(-float(rows) * rate)
    begun = [info_ref[BEGUN.start + i * CHUNKS : BEGUN.start + i * CHUNKS + held, :] for i in range(3)]
    for rank in range(ranks):
        kept = whole
        for begin in begun:
            kept = jnp.where(begin == float(rank), 0.0, kept)
        out_ref[rank] = kept


def scan_kernel(factor_ref, pieces_ref, out_ref):
    running = jnp.zeros(pieces_ref.shape[1:], F32)
    for rank in range(pieces_ref.shape[0]):
        out_ref[rank] = running
        running = factor_ref[rank] * running + pieces_ref[rank]


def near_kernel(rows, poles, first, early, info_ref, rim_ref, taps_ref, rate_ref, gain_ref, skip_ref, gated_in, q_in, r_in, q_hbm, res_hbm, gated_hbm, *others):
    if early:
        outs, (factor_ref, gated_next, q_next, r_next, *others) = others[:3], others[3:]
        near_ref, query_ref, local_ref, q_ref, r_ref, qx, rx, decay_ref, own_sems, far_sems, next_sems = others
        gated_ref = gated_in
        count = near_ref.shape[0]
    else:
        heads, tails, others = others[:3], others[3:6], others[6:]
        gated_ref, near_ref, query_ref, local_ref, q_ref, r_ref, qx, rx, decay_ref, own_sems, far_sems = others
        count = near_ref.shape[0]

    def fetch(here):
        pairs = [(q_hbm.at[:, lanes_at(first + here)], q_ref.at[:, lanes_at(here)])]
        pairs.append((res_hbm.at[:, lanes_at(first + here)], r_ref.at[:, lanes_at(here)]))
        if not early:
            pairs.append((gated_hbm.at[here], gated_ref.at[here]))
        return [
            pltpu.make_async_copy(source, target, own_sems.at[i, here])
            for i, (source, target) in enumerate(pairs)
        ]

    for here in range(HEAD, count):
        for copy in fetch(here):
            copy.start()
    for i, (source, target) in enumerate(((q_in, q_ref), (r_in, r_ref))):
        target[:, : HEAD * LANES] = source[...]
    if early:
        columns = pl.ds((first + count) * LANES, HEAD * LANES)
        pairs = (
            (gated_hbm.at[pl.ds(0, HEAD)], gated_next),
            (q_hbm.at[:, columns], q_next),
            (res_hbm.at[:, columns], r_next),
        )
        ahead_of_time = [
            pltpu.make_async_copy(source, target, next_sems.at[i]) for i, (source, target) in enumerate(pairs)
        ]
        for copy in ahead_of_time:
            copy.start()
        rank_factors(info_ref, rows, poles, rate_ref, factor_ref)
    else:
        gated_ref[:HEAD] = gated_in[...]
    span = rows // CHUNKS
    chunk = lax.broadcasted_iota(jnp.int32, (CHUNKS, LANES), 0)
    flags = [
        jnp.max(info_ref[FLAGS.start + block : FLAGS.start + block + 1, :]) > 0.0
        for block in range(span // STEPS)
    ]

    made = (near_ref, query_ref, local_ref)

    def store(here, targets, low):
        return [
            pltpu.make_async_copy(source.at[here], target.at[here - low], far_sems.at[i, here])
            for i, (source, target) in enumerate(zip(made, targets))
        ]

    @pl.loop(0, count)
    def _(here):
        own = lanes_at(here)
        lanes = lanes_at(here + first)
        far = info_ref[FAR, :]
        joined = info_ref[JOINED, :]

        @pl.when(here >= HEAD)
        def _():
            for copy in fetch(here):
                copy.wait()

        qx[5:7, :] = rim_ref[:, lanes].astype(F32)
        lay_out(q_ref, own, qx, span, 8)
        lay_out(r_ref, own, rx, span, 0)
        decay_ref[...] = jnp.exp(-rate_ref[:, lanes])
        taps = [spread(taps_ref[j : j + 1, lanes]) for j in range(3)]
        skip = spread(skip_ref[:, lanes])
        decay = [spread(decay_ref[m : m + 1, :]) for m in range(poles)]
        gain = [spread(gain_ref[m : m + 1, lanes]) for m in range(poles)]
        carry = [
            qx[pl.ds(6, CHUNKS, stride=span + 1), :],
            qx[pl.ds(5, CHUNKS, stride=span + 1), :] * far,
        ] + [jnp.zeros((CHUNKS, LANES), F32)] * poles

        def run(block, masked, carry):
            carry = list(carry)
            for step in range(STEPS):
                place = block * STEPS + step
                if masked:
                    keep = jnp.ones((CHUNKS, LANES), F32)
                    for i in range(3):
                        low = INSIDE.start + i * CHUNKS
                        keep = jnp.where(info_ref[low : low + CHUNKS, :] == float(place), 0.0, keep)
                    carry = [held * keep for held in carry]
                query = qx[pl.ds(8 + place, CHUNKS, stride=span + 1), :]
                query_short = taps[0] * query + taps[1] * carry[0] + taps[2] * carry[1]
                gated = gated_ref[here, pl.ds(place, CHUNKS, stride=span + 1), :]
                states = [decay[m] * carry[2 + m] + gated for m in range(poles)]
                total = skip * gated
                for m in range(poles):
                    total = total + gain[m] * states[m]
                query_ref[here, chunk_of(place), :] = query_short
                near_ref[here, chunk_of(place), :] = (
                    rx[pl.ds(place, CHUNKS, stride=span + 1), :] + query_short * total
                )
                carry = [query, carry[0]] + states
            return tuple(carry)

        carry = walk(span, flags, run, tuple(carry))
        for m in range(poles):
            reach = jnp.exp(-float(span) * spread(rate_ref[m : m + 1, lanes])) * joined
            state = carry[2 + m]
            for hop in (1, 2, 4):
                state = state + reach * pltpu.roll(state, hop, 0)
                if hop < 4:
                    reach = reach * pltpu.roll(reach, hop, 0)
            local_ref[here, m * CHUNKS : (m + 1) * CHUNKS, :] = jnp.where(
                chunk > 0, pltpu.roll(state, 1, 0), 0.0
            )
        if early:
            for copy in store(here, outs, 0):
                copy.start()
        else:

            @pl.when(here < READY)
            def _():
                for source, target in zip(made, heads):
                    target[here] = source[here]

            @pl.when(here >= READY)
            def _():
                for copy in store(here, tails, READY):
                    copy.start()

    if early:
        for copy in ahead_of_time:
            copy.wait()
    for here in range(0 if early else READY, count):
        for copy in store(here, outs, 0) if early else store(here, tails, READY):
            copy.wait()


def stream_kernel(rows, poles, info_ref, rate_ref, gain_ref, incoming_ref, near_hbm, query_hbm, local_hbm, near_head, query_head, local_head, near_rest, query_rest, local_rest, out_hbm, stream_ref, power_ref, near_a, query_a, local_a, near_b, query_b, local_b, sx, px, decay_ref, sems, far_sems, rest_sems):
    span = rows // CHUNKS
    chunk = lax.broadcasted_iota(jnp.int32, (CHUNKS, LANES), 0)
    px[...] = jnp.zeros_like(px)
    inner = GROUP // LANES
    early = near_a.shape[0]

    def fetch(group):
        here = pl.ds(group * inner, inner)
        pairs = ((near_hbm, near_a), (query_hbm, query_a), (local_hbm, local_a))
        return [
            pltpu.make_async_copy(source.at[here], target.at[here], far_sems.at[i, group])
            for i, (source, target) in enumerate(pairs)
        ]

    pairs = ((near_rest, near_b), (query_rest, query_b), (local_rest, local_b))
    rest = [pltpu.make_async_copy(source, target, rest_sems.at[i]) for i, (source, target) in enumerate(pairs)]
    for group in range(early // inner):
        for copy in fetch(group):
            copy.start()
    for copy in rest:
        copy.start()
    before = (chunk * span).astype(F32)

    def copy_out(group):
        lanes = pl.ds(pl.multiple_of(group * GROUP, GROUP), GROUP)
        return pltpu.make_async_copy(stream_ref.at[:, lanes], out_hbm.at[:, lanes], sems.at[group])

    def one_part(part, near_ref, query_ref, local_ref, place_of):
        lanes = lanes_at(part)
        decay_ref[...] = jnp.exp(-rate_ref[:, lanes])
        decay = [spread(decay_ref[m : m + 1, :]) for m in range(poles)]
        reached = info_ref[REACHED, :]
        ahead = info_ref[AHEAD, :]
        carry = []
        for m in range(poles):
            entering = reached * jnp.exp(-before * spread(rate_ref[m : m + 1, lanes]))
            entering = entering * spread(incoming_ref[part, m : m + 1, :])
            entering = entering + local_ref[place_of, m * CHUNKS : (m + 1) * CHUNKS, :]
            carry.append(spread(gain_ref[m : m + 1, lanes]) * entering)
        for place in range(span):
            carry = [decay[m] * carry[m] for m in range(poles)]
            terms = list(carry)
            while len(terms) > 1:
                terms = [
                    terms[i] + terms[i + 1] if i + 1 < len(terms) else terms[i]
                    for i in range(0, len(terms), 2)
                ]
            carried = jnp.where(ahead > float(place), terms[0], 0.0)
            here = chunk_of(place)
            sx[pl.ds(place, CHUNKS, stride=span + 1), :] = (
                near_ref[place_of, here, :] + query_ref[place_of, here, :] * carried
            )
        for piece in range(CHUNKS):
            low = piece * (span + 1)
            stream = sx[low : low + span, :]
            native = slice(piece * span, (piece + 1) * span)
            stream_ref[native, lanes] = stream
            px[native, :] += stream * stream

    groups = stream_ref.shape[1] // GROUP
    sides = (
        (early, near_head, query_head, local_head),
        (0, near_a, query_a, local_a),
        (early + READY, near_b, query_b, local_b),
    )
    for first, near_ref, query_ref, local_ref in sides:

        @pl.loop(0, near_ref.shape[0] // inner)
        def _(group):
            if near_ref is near_a:
                for copy in fetch(group):
                    copy.wait()
            if near_ref is near_b:
                for copy in rest:
                    copy.wait()

            @pl.loop(group * inner, (group + 1) * inner)
            def _(part):
                one_part(part + first, near_ref, query_ref, local_ref, part)

            copy_out(group + first // inner).start()

    for piece in range(rows // LANES):
        turned = px[piece * LANES : (piece + 1) * LANES, :].T
        power_ref[piece : piece + 1, :] = jnp.sum(turned, axis=0, keepdims=True)
    for group in range(groups):
        copy_out(group).wait()


def norm_kernel(width, power_ref, gain_ref, stream_ref, out_hbm, scale_ref, buffer, sems):
    scale = lax.rsqrt(jnp.sum(power_ref[...], axis=0) / width + 1e-06)
    for piece in range(scale.shape[0]):
        wide = jnp.broadcast_to(scale[piece : piece + 1, :], (LANES, LANES))
        scale_ref[piece * LANES : (piece + 1) * LANES, :] = wide.T
    rows = stream_ref.shape[0]
    count = sems.shape[0]
    tall = rows // count

    def copy_out(group):
        here = pl.ds(pl.multiple_of(group * tall, tall), tall)
        return pltpu.make_async_copy(buffer.at[here, :], out_hbm.at[here, :], sems.at[group])

    @pl.loop(0, count)
    def _(group):
        here = pl.ds(pl.multiple_of(group * tall, tall), tall)
        factor = scale_ref[here, :]
        for part in range(stream_ref.shape[1] // LANES):
            lanes = slice(part * LANES, (part + 1) * LANES)
            buffer[here, lanes] = stream_ref[here, lanes] * factor * gain_ref[:, lanes]
        copy_out(group).start()

    for group in range(count):
        copy_out(group).wait()


def shifted(block, axis, distance, wrap):
    count = lax.axis_size(axis)
    route = [(i, (i + distance) % count) for i in range(count) if wrap or i + distance < count]
    return lax.ppermute(block, axis, route)


def on_device(query_proj, key_proj, value_proj, short_filter, decay_rate, residue, skip_gain, norm_gain, residual, lengths):
    rows, width = query_proj.shape
    poles = decay_rate.shape[0]
    ranks = lax.axis_size("ctx")
    parts = width // LANES
    groups = width // GROUP
    near_by = pl.BlockSpec(memory_space=pltpu.VMEM)
    outside = pl.BlockSpec(memory_space=pltpu.HBM)
    limit = pltpu.CompilerParams(vmem_limit_bytes=12 * 1024 * 1024)
    shape = lambda *dims: jax.ShapeDtypeStruct(dims, F32)
    kept_near = lambda *dims: pltpu.VMEM(dims, F32)
    far_off = lambda array: pltpu.with_memory_space_constraint(array, pltpu.HBM)
    close_by = lambda array: pltpu.with_memory_space_constraint(array, pltpu.VMEM)
    query_proj, key_proj, value_proj, residual, short_filter, lengths = map(
        far_off, (query_proj, key_proj, value_proj, residual, short_filter, lengths)
    )

    rims = pl.pallas_call(
        rim_kernel,
        in_specs=[outside] * 3,
        out_specs=near_by,
        out_shape=pltpu.VMEM((3, 2, width), BF16),
        scratch_shapes=[pltpu.VMEM((3, 16, width), BF16), pltpu.SemaphoreType.DMA((3,))],
        name="rims",
    )(query_proj, key_proj, value_proj)
    rims = shifted(rims, "ctx", 1, False)
    pole_gain = residue * jnp.sqrt(-jnp.expm1(-2.0 * decay_rate))
    skip = skip_gain.reshape(1, width)

    early = FIRST_SHARE * (GROUP // LANES)
    late = parts - early
    pitch = rows + CHUNKS
    held = parts * poles // ranks
    gated_a, gated_b, end, q_a, r_a, query_rim, query_taps, info = pl.pallas_call(
        functools.partial(end_kernel, rows, poles),
        in_specs=[outside] * 5 + [near_by, outside, outside],
        out_specs=[near_by, outside, outside] + [near_by] * 5,
        out_shape=[
            kept_near(early, pitch, LANES),
            pltpu.HBM((late, pitch, LANES), F32),
            pltpu.HBM((parts, poles, LANES), F32),
            pltpu.VMEM((rows, HEAD * LANES), BF16),
            pltpu.VMEM((rows, HEAD * LANES), BF16),
            pltpu.VMEM((2, width), BF16),
            kept_near(3, width),
            kept_near(SECTIONS, LANES),
        ],
        scratch_shapes=[
            pltpu.SMEM(lengths.shape, jnp.int32),
            pltpu.VMEM((rows, width), BF16),
            pltpu.VMEM((rows, width), BF16),
            pltpu.VMEM((late, pitch, LANES), F32),
            pltpu.VMEM((parts, poles, LANES), F32),
            pltpu.VMEM((3, 3, width), F32),
            pltpu.VMEM((poles, width), F32),
            pltpu.VMEM((rows + 8, LANES), F32),
            pltpu.VMEM((rows + 8, LANES), F32),
            pltpu.VMEM((rows, LANES), F32),
            pltpu.VMEM((poles, LANES), F32),
            pltpu.SemaphoreType.DMA((2, groups)),
            pltpu.SemaphoreType.DMA((late,)),
            pltpu.SemaphoreType.DMA((groups,)),
            pltpu.SemaphoreType.DMA((5,)),
        ],
        compiler_params=limit,
        name="end_state",
    )(lengths, key_proj, value_proj, query_proj, residual, rims, short_filter, decay_rate)
    info, query_rim, query_taps = map(close_by, (info, query_rim, query_taps))

    pieces = lax.all_to_all(end.reshape(ranks, held, LANES), "ctx", 0, 0, tiled=True)

    def near_side(first, count, gated, q_part, r_part, early):
        block = (count, rows, LANES)
        states = (count, poles * CHUNKS, LANES)
        given = [info, query_rim, query_taps, decay_rate, pole_gain, skip, *map(close_by, (gated, q_part, r_part))]
        fetched = [query_proj, residual, far_off(gated_b)]
        scratch = [
            pltpu.VMEM((rows, count * LANES), BF16),
            pltpu.VMEM((rows, count * LANES), BF16),
            pltpu.VMEM((rows + 16, LANES), F32),
            pltpu.VMEM((rows + 16, LANES), F32),
            pltpu.VMEM((poles, LANES), F32),
            pltpu.SemaphoreType.DMA((3, count)),
            pltpu.SemaphoreType.DMA((3, count)),
        ]
        if early:
            out_specs = [outside] * 3 + [near_by] * 4
            out_shape = [pltpu.HBM(dims, F32) for dims in (block, block, states)] + [
                kept_near(ranks, held, LANES),
                kept_near(HEAD, pitch, LANES),
                pltpu.VMEM((rows, HEAD * LANES), BF16),
                pltpu.VMEM((rows, HEAD * LANES), BF16),
            ]
            scratch = [pltpu.VMEM(dims, F32) for dims in (block, block, states)] + scratch
            scratch += [pltpu.SemaphoreType.DMA((3,))]
        else:
            out_specs = [near_by] * 3 + [outside] * 3
            out_shape = [kept_near(READY, *dims[1:]) for dims in (block, block, states)]
            out_shape += [pltpu.HBM((count - READY, *dims[1:]), F32) for dims in (block, block, states)]
            scratch = [pltpu.VMEM(dims, F32) for dims in ((count, pitch, LANES), block, block, states)] + scratch
        return pl.pallas_call(
            functools.partial(near_kernel, rows, poles, first, early),
            in_specs=[near_by] * len(given) + [outside] * len(fetched),
            out_specs=out_specs,
            out_shape=out_shape,
            scratch_shapes=scratch,
            compiler_params=limit,
            cost_estimate=pl.CostEstimate(flops=4000000, bytes_accessed=8000000, transcendentals=0),
            name="near",
        )(*given, *fetched)

    near_a, query_a, local_a, factors, gated_head, q_b, r_b = near_side(0, early, gated_a, q_a, r_a, True)
    near_b = near_side(early, late, gated_head, q_b, r_b, False)
    scanned = pl.pallas_call(
        scan_kernel,
        in_specs=[near_by, near_by],
        out_specs=near_by,
        out_shape=pltpu.HBM((ranks, held, LANES), F32),
        compiler_params=limit,
        name="rank_scan",
    )(close_by(factors), pieces)
    incoming = lax.all_to_all(scanned, "ctx", 0, 0, tiled=True).reshape(parts, poles, LANES)

    stream, kept, power = pl.pallas_call(
        functools.partial(stream_kernel, rows, poles),
        in_specs=[near_by] * 4 + [outside] * 3 + [near_by] * 3 + [outside] * 3,
        out_specs=[outside, near_by, near_by],
        out_shape=[pltpu.HBM((rows, width), F32), kept_near(rows, width), kept_near(rows // LANES, LANES)],
        scratch_shapes=[
            pltpu.VMEM((early, rows, LANES), F32),
            pltpu.VMEM((early, rows, LANES), F32),
            pltpu.VMEM((early, poles * CHUNKS, LANES), F32),
            pltpu.VMEM((late - READY, rows, LANES), F32),
            pltpu.VMEM((late - READY, rows, LANES), F32),
            pltpu.VMEM((late - READY, poles * CHUNKS, LANES), F32),
            pltpu.VMEM((rows + 8, LANES), F32),
            pltpu.VMEM((rows, LANES), F32),
            pltpu.VMEM((poles, LANES), F32),
            pltpu.SemaphoreType.DMA((groups,)),
            pltpu.SemaphoreType.DMA((3, early // (GROUP // LANES))),
            pltpu.SemaphoreType.DMA((3,)),
        ],
        compiler_params=limit,
        name="stream",
    )(
        info,
        decay_rate,
        pole_gain,
        incoming,
        *map(far_off, (near_a, query_a, local_a)),
        *map(close_by, near_b[:3]),
        *map(far_off, near_b[3:]),
    )
    shares = lax.axis_size("ch")
    powers = jnp.stack([power] + [shifted(power, "ch", i, True) for i in range(1, shares)])
    normed = pl.pallas_call(
        functools.partial(norm_kernel, float(width * shares)),
        in_specs=[near_by, near_by, near_by],
        out_specs=outside,
        out_shape=shape(rows, width),
        scratch_shapes=[
            pltpu.VMEM((rows, LANES), F32),
            pltpu.VMEM((rows, width), F32),
            pltpu.SemaphoreType.DMA((8,)),
        ],
        compiler_params=limit,
        name="norm",
    )(powers, norm_gain.reshape(1, width), close_by(kept))
    return (stream, normed)


def solution(mesh):
    placed = (
        P("ctx", "ch"),
        P("ctx", "ch"),
        P("ctx", "ch"),
        P(None, None, "ch"),
        P(None, "ch"),
        P(None, "ch"),
        P("ch"),
        P("ch"),
        P("ctx", "ch"),
        P(),
    )
    return jax.shard_map(
        on_device,
        mesh=mesh,
        in_specs=placed,
        out_specs=(P("ctx", "ch"), P("ctx", "ch")),
        check_vma=False,
    )
```

```python
import functools

import jax
import jax.numpy as jnp
from jax import lax
from jax.experimental import pallas as pl
from jax.experimental.pallas import tpu as pltpu
from jax.sharding import PartitionSpec as P

LANES = 128
CHUNKS = 8
GROUP = 256
FIRST_SHARE = 4
HEAD = 2
NEXT = 4
READY = 6
STEPS = 16
F32 = jnp.float32
BF16 = jnp.bfloat16


def starts_of(lengths_ref):
    first = lengths_ref[0]
    second = first + lengths_ref[1]
    third = second + lengths_ref[2]
    return (first, second, third)


def spread(row):
    return jnp.broadcast_to(row, (CHUNKS, LANES))


def no_start(starts, where):
    kept = jnp.ones(where.shape, jnp.bool_)
    for start in starts:
        kept = kept & (where != start)
    return kept.astype(F32)


def any_in(starts, low, high):
    found = jnp.bool_(False)
    for start in starts:
        found = found | ((start >= low) & (start < high))
    return found


def block_has_start(starts, base, rows, block):
    found = jnp.bool_(False)
    for start in starts:
        inside = start - base
        place = lax.rem(jnp.maximum(inside, 0), rows // CHUNKS)
        found = found | (
            (inside >= 0) & (inside < rows) & (place >= block * STEPS) & (place < (block + 1) * STEPS)
        )
    return found


def lanes_at(part):
    return pl.ds(pl.multiple_of(part * LANES, LANES), LANES)


def chunk_of(place):
    return pl.ds(pl.multiple_of(place * CHUNKS, CHUNKS), CHUNKS)


def lay_out(source, lanes, target, span, offset):
    for piece in range(CHUNKS):
        low = offset + piece * (span + 1)
        target[low : low + span, :] = source[piece * span : (piece + 1) * span, lanes].astype(F32)


def rim_kernel(q_hbm, k_hbm, v_hbm, out_ref, buffer, sems):
    tail = buffer.shape[1]
    copies = [
        pltpu.make_async_copy(source.at[pl.ds(source.shape[0] - tail, tail), :], buffer.at[i], sems.at[i])
        for i, source in enumerate((q_hbm, k_hbm, v_hbm))
    ]
    for copy in copies:
        copy.start()
    for i, copy in enumerate(copies):
        copy.wait()
        out_ref[i] = buffer[i, tail - 2 :, :]


def walk(span, flags, run, carry):
    for block in range(span // STEPS):
        carry = lax.cond(
            flags[block], functools.partial(run, block, True), functools.partial(run, block, False), carry
        )
    return carry


FAR, JOINED, REACHED, AHEAD, FLAGS, BEGUN, INSIDE = (slice(i * CHUNKS, (i + 1) * CHUNKS) for i in (0, 1, 2, 3, 4, 5, 8))
SECTIONS = 11 * CHUNKS


def describe(starts, base, rows, info_ref):
    span = rows // CHUNKS
    chunk = lax.broadcasted_iota(jnp.int32, (CHUNKS, LANES), 0)
    chunk_row = base + chunk * span
    alive = jnp.ones((CHUNKS, LANES), jnp.bool_)
    reached = jnp.ones((CHUNKS, LANES), jnp.bool_)
    ahead = jnp.full((CHUNKS, LANES), span, jnp.int32)
    for start in starts:
        inside = start - chunk_row
        alive = alive & ((inside < 0) | (inside >= span))
        reached = reached & ((start < base) | (inside >= 0))
        ahead = jnp.where((inside >= 0) & (inside < ahead), inside, ahead)
    info_ref[FAR, :] = no_start(starts, chunk_row - 1)
    info_ref[JOINED, :] = (alive & (chunk > 0)).astype(F32)
    info_ref[REACHED, :] = reached.astype(F32)
    info_ref[AHEAD, :] = ahead.astype(F32)
    for block in range(span // STEPS):
        flag = jnp.where(block_has_start(starts, base, rows, block), 1.0, 0.0)
        info_ref[FLAGS.start + block : FLAGS.start + block + 1, :] = jnp.full((1, LANES), flag, F32)
    for i, start in enumerate(starts):
        rank = lax.div(start, rows).astype(F32)
        low = BEGUN.start + i * CHUNKS
        info_ref[low : low + CHUNKS, :] = jnp.full((CHUNKS, LANES), rank, F32)
        low = INSIDE.start + i * CHUNKS
        info_ref[low : low + CHUNKS, :] = (start - chunk_row).astype(F32)


def pitched(row, span):
    return row + lax.div(row, span)


def fetch_kernel(rows, lengths_hbm, k_hbm, v_hbm, q_hbm, res_hbm, taps_hbm, k_ref, v_ref, q_next, r_next, taps_ref, info_ref, lengths_ref, sems):
    columns = pl.ds(0, q_next.shape[1])
    pairs = (
        (lengths_hbm, lengths_ref),
        (k_hbm, k_ref),
        (v_hbm, v_ref),
        (q_hbm.at[:, columns], q_next),
        (res_hbm.at[:, columns], r_next),
        (taps_hbm, taps_ref),
    )
    copies = [pltpu.make_async_copy(source, target, sems.at[i]) for i, (source, target) in enumerate(pairs)]
    for copy in copies:
        copy.start()
    copies[0].wait()
    describe(starts_of(lengths_ref), lax.axis_index("ctx") * rows, rows, info_ref)
    for copy in copies[1:]:
        copy.wait()


def end_kernel(rows, poles, info_ref, k_ref, v_ref, rim_ref, taps_ref, rate_ref, gated_a, gated_hbm, end_hbm, rim_next, taps_next, gated_b, end_ref, kx, vx, gx, decay_ref, mends, out_sems, end_sems):
    span = rows // CHUNKS
    phase = lax.broadcasted_iota(jnp.int32, (CHUNKS, LANES), 0)
    groups = k_ref.shape[1] // GROUP
    rim_next[...] = rim_ref[0]
    taps_next[...] = taps_ref[0]
    last = jnp.int32(0)
    mended = jnp.int32(0)
    for i in range(3):
        low = INSIDE.start + i * CHUNKS
        inside = jnp.max(info_ref[low : low + 1, :]).astype(jnp.int32)
        here_now = (inside >= 0) & (inside < rows)
        last = jnp.where(here_now, inside, last)
        for row, reach, wanted in (
            (inside, 0, here_now),
            (inside + 1, 1, (inside >= -1) & (inside < rows - 1)),
        ):
            mends[0, mended] = jnp.where(wanted, row, 0)
            mends[1, mended] = reach
            mended = mended + wanted.astype(jnp.int32)
    inner = GROUP // LANES

    def store(here):
        return pltpu.make_async_copy(gated_b.at[here], gated_hbm.at[here], out_sems.at[here])

    def send(group):
        here = pl.ds(group * inner, inner)
        return pltpu.make_async_copy(end_ref.at[here], end_hbm.at[here], end_sems.at[group])

    def one_group(group, first, gated_ref):
        @pl.loop(group * inner, (group + 1) * inner)
        def _(part):
            lanes = lanes_at(part)
            here = part - first * inner
            for i, source, target in ((1, k_ref, kx), (2, v_ref, vx)):
                target[6:8, :] = rim_ref[i, :, lanes].astype(F32)
                target[8:, :] = source[:, lanes].astype(F32)
            decay_ref[...] = jnp.exp(-float(CHUNKS) * rate_ref[:, lanes])
            lines = [[taps_ref[i, j : j + 1, lanes] for j in range(3)] for i in (1, 2)]
            taps = [[spread(line) for line in three] for three in lines]
            for block in range(rows // CHUNKS):
                low = block * CHUNKS
                shorts = []
                for three, source in zip(taps, (kx, vx)):
                    short = three[0] * source[low + 8 : low + 16, :]
                    for back in (1, 2):
                        short = short + three[back] * source[low + 8 - back : low + 16 - back, :]
                    shorts.append(short)
                gated = shorts[0] * shorts[1]
                gx[low : low + CHUNKS, :] = gated
                to = low + low // span
                gated_ref[here, to : to + CHUNKS, :] = gated

            @pl.when(mended > 0)
            def _():
                @pl.loop(0, mended)
                def _(i):
                    row = mends[0, i]
                    reach = mends[1, i].astype(F32)
                    shorts = []
                    for three, source in zip(lines, (kx, vx)):
                        now = three[0] * source[pl.ds(row + 8, 1), :]
                        shorts.append(now + three[1] * source[pl.ds(row + 7, 1), :] * reach)
                    gated = shorts[0] * shorts[1]
                    gx[pl.ds(row, 1), :] = gated
                    gated_ref[here, pl.ds(pitched(row, span), 1), :] = gated

                for block in range(rows // CHUNKS):
                    low = block * CHUNKS
                    gx[low : low + CHUNKS, :] = jnp.where(
                        phase + low >= last, gx[low : low + CHUNKS, :], 0.0
                    )

            decay = [spread(decay_ref[m : m + 1, :]) for m in range(poles)]
            sums = [gx[:CHUNKS, :] for _ in range(poles)]
            for block in range(1, rows // CHUNKS):
                gated = gx[block * CHUNKS : (block + 1) * CHUNKS, :]
                sums = [decay[m] * sums[m] + gated for m in range(poles)]
            after = (phase - (CHUNKS - 1)).astype(F32)
            for m in range(poles):
                weight = jnp.exp(after * spread(rate_ref[m : m + 1, lanes]))
                end_ref[part, m : m + 1, :] = jnp.sum(weight * sums[m], axis=0, keepdims=True)
            if first:
                store(here).start()

        send(group).start()

    middle = gated_a.shape[0] // inner
    pl.loop(middle, groups)(lambda group: one_group(group, middle, gated_b))
    pl.loop(0, middle)(lambda group: one_group(group, 0, gated_a))
    for here in range(gated_b.shape[0]):
        store(here).wait()
    for group in range(groups):
        send(group).wait()


def rank_factors(info_ref, rows, poles, rate_ref, out_ref):
    ranks, held = out_ref.shape[:2]
    shares = poles // held
    mine = lax.axis_index("ctx")
    lanes = lanes_at(lax.div(mine, shares))
    rate = rate_ref[:held, lanes]
    for share in range(1, shares):
        theirs = rate_ref[share * held : (share + 1) * held, lanes]
        rate = jnp.where(lax.rem(mine, shares) == share, theirs, rate)
    whole = jnp.exp(-float(rows) * rate)
    begun = [info_ref[BEGUN.start + i * CHUNKS : BEGUN.start + i * CHUNKS + held, :] for i in range(3)]
    for rank in range(ranks):
        kept = whole
        for begin in begun:
            kept = jnp.where(begin == float(rank), 0.0, kept)
        out_ref[rank] = kept


def scan_kernel(factor_ref, pieces_ref, out_hbm, out_ref, sems):
    running = jnp.zeros(pieces_ref.shape[1:], F32)
    ranks = pieces_ref.shape[0]
    block = ranks // sems.shape[0]
    copies = []
    for rank in range(ranks):
        out_ref[rank] = running
        running = factor_ref[rank] * running + pieces_ref[rank]
        if rank % block == block - 1:
            here = pl.ds(rank - block + 1, block)
            copies.append(pltpu.make_async_copy(out_ref.at[here], out_hbm.at[here], sems.at[rank // block]))
            copies[-1].start()
    for copy in copies:
        copy.wait()


def near_kernel(rows, poles, first, early, info_ref, rim_ref, taps_ref, rate_ref, gain_ref, skip_ref, gated_in, q_in, r_in, q_hbm, res_hbm, gated_hbm, *others):
    if early:
        outs, (factor_ref, gated_next, q_next, r_next, *others) = others[:3], others[3:]
        near_ref, query_ref, local_ref, q_ref, r_ref, qx, rx, decay_ref, own_sems, far_sems, next_sems = others
        gated_ref = gated_in
        count = near_ref.shape[0]
    else:
        heads, tails, others = others[:3], others[3:6], others[6:]
        gated_ref, near_ref, query_ref, local_ref, q_ref, r_ref, qx, rx, decay_ref, own_sems, far_sems = others
        count = near_ref.shape[0]

    cuts = ((HEAD, NEXT), (NEXT, count))

    def fetch(cut):
        low, high = cuts[cut]
        from_columns = pl.ds((first + low) * LANES, (high - low) * LANES)
        columns = pl.ds(low * LANES, (high - low) * LANES)
        pairs = [(source.at[:, from_columns], target.at[:, columns]) for source, target in ((q_hbm, q_ref), (res_hbm, r_ref))]
        if not early:
            blocks = pl.ds(low, high - low)
            pairs.append((gated_hbm.at[blocks], gated_ref.at[blocks]))
        return [
            pltpu.make_async_copy(source, target, own_sems.at[i, cut])
            for i, (source, target) in enumerate(pairs)
        ]

    for cut in range(len(cuts)):
        for copy in fetch(cut):
            copy.start()
    for i, (source, target) in enumerate(((q_in, q_ref), (r_in, r_ref))):
        target[:, : HEAD * LANES] = source[...]
    if early:
        columns = pl.ds((first + count) * LANES, HEAD * LANES)
        pairs = (
            (gated_hbm.at[pl.ds(0, HEAD)], gated_next),
            (q_hbm.at[:, columns], q_next),
            (res_hbm.at[:, columns], r_next),
        )
        ahead_of_time = [
            pltpu.make_async_copy(source, target, next_sems.at[i]) for i, (source, target) in enumerate(pairs)
        ]
        for copy in ahead_of_time:
            copy.start()
        rank_factors(info_ref, rows, poles, rate_ref, factor_ref)
    else:
        gated_ref[:HEAD] = gated_in[...]
    span = rows // CHUNKS
    chunk = lax.broadcasted_iota(jnp.int32, (CHUNKS, LANES), 0)
    flags = [
        jnp.max(info_ref[FLAGS.start + block : FLAGS.start + block + 1, :]) > 0.0
        for block in range(span // STEPS)
    ]

    made = (near_ref, query_ref, local_ref)

    def store(here, targets, low):
        return [
            pltpu.make_async_copy(source.at[here], target.at[here - low], far_sems.at[i, here])
            for i, (source, target) in enumerate(zip(made, targets))
        ]

    @pl.loop(0, count)
    def _(here):
        own = lanes_at(here)
        lanes = lanes_at(here + first)
        far = info_ref[FAR, :]
        joined = info_ref[JOINED, :]

        for cut, (low, _) in enumerate(cuts):

            @pl.when(here == low)
            def _():
                for copy in fetch(cut):
                    copy.wait()

        qx[5:7, :] = rim_ref[:, lanes].astype(F32)
        lay_out(q_ref, own, qx, span, 8)
        lay_out(r_ref, own, rx, span, 0)
        decay_ref[...] = jnp.exp(-rate_ref[:, lanes])
        taps = [spread(taps_ref[j : j + 1, lanes]) for j in range(3)]
        skip = spread(skip_ref[:, lanes])
        decay = [spread(decay_ref[m : m + 1, :]) for m in range(poles)]
        gain = [spread(gain_ref[m : m + 1, lanes]) for m in range(poles)]
        carry = [
            qx[pl.ds(6, CHUNKS, stride=span + 1), :],
            qx[pl.ds(5, CHUNKS, stride=span + 1), :] * far,
        ] + [jnp.zeros((CHUNKS, LANES), F32)] * poles

        def run(block, masked, carry):
            carry = list(carry)
            for step in range(STEPS):
                place = block * STEPS + step
                if masked:
                    keep = jnp.ones((CHUNKS, LANES), F32)
                    for i in range(3):
                        low = INSIDE.start + i * CHUNKS
                        keep = jnp.where(info_ref[low : low + CHUNKS, :] == float(place), 0.0, keep)
                    carry = [held * keep for held in carry]
                query = qx[pl.ds(8 + place, CHUNKS, stride=span + 1), :]
                query_short = taps[0] * query + taps[1] * carry[0] + taps[2] * carry[1]
                gated = gated_ref[here, pl.ds(place, CHUNKS, stride=span + 1), :]
                states = [decay[m] * carry[2 + m] + gated for m in range(poles)]
                total = skip * gated
                for m in range(poles):
                    total = total + gain[m] * states[m]
                query_ref[here, chunk_of(place), :] = query_short
                near_ref[here, chunk_of(place), :] = (
                    rx[pl.ds(place, CHUNKS, stride=span + 1), :] + query_short * total
                )
                carry = [query, carry[0]] + states
            return tuple(carry)

        carry = walk(span, flags, run, tuple(carry))
        for m in range(poles):
            reach = jnp.exp(-float(span) * spread(rate_ref[m : m + 1, lanes])) * joined
            state = carry[2 + m]
            for hop in (1, 2, 4):
                state = state + reach * pltpu.roll(state, hop, 0)
                if hop < 4:
                    reach = reach * pltpu.roll(reach, hop, 0)
            local_ref[here, m * CHUNKS : (m + 1) * CHUNKS, :] = jnp.where(
                chunk > 0, pltpu.roll(state, 1, 0), 0.0
            )
        if early:
            for copy in store(here, outs, 0):
                copy.start()
        else:

            @pl.when(here < READY)
            def _():
                for source, target in zip(made, heads):
                    target[here] = source[here]

            @pl.when(here >= READY)
            def _():
                for copy in store(here, tails, READY):
                    copy.start()

    if early:
        for copy in ahead_of_time:
            copy.wait()
    for here in range(0 if early else READY, count):
        for copy in store(here, outs, 0) if early else store(here, tails, READY):
            copy.wait()


def stream_kernel(rows, poles, info_ref, rate_ref, gain_ref, incoming_ref, near_hbm, query_hbm, local_hbm, near_head, query_head, local_head, near_rest, query_rest, local_rest, out_hbm, stream_ref, power_ref, near_a, query_a, local_a, near_b, query_b, local_b, sx, px, decay_ref, sems, far_sems, rest_sems):
    span = rows // CHUNKS
    chunk = lax.broadcasted_iota(jnp.int32, (CHUNKS, LANES), 0)
    px[...] = jnp.zeros_like(px)
    inner = GROUP // LANES
    early = near_a.shape[0]

    def fetch(group):
        here = pl.ds(group * inner, inner)
        pairs = ((near_hbm, near_a), (query_hbm, query_a), (local_hbm, local_a))
        return [
            pltpu.make_async_copy(source.at[here], target.at[here], far_sems.at[i, group])
            for i, (source, target) in enumerate(pairs)
        ]

    pairs = ((near_rest, near_b), (query_rest, query_b), (local_rest, local_b))
    rest = [pltpu.make_async_copy(source, target, rest_sems.at[i]) for i, (source, target) in enumerate(pairs)]
    for group in range(early // inner):
        for copy in fetch(group):
            copy.start()
    for copy in rest:
        copy.start()
    before = (chunk * span).astype(F32)

    def copy_out(group):
        lanes = pl.ds(pl.multiple_of(group * GROUP, GROUP), GROUP)
        return pltpu.make_async_copy(stream_ref.at[:, lanes], out_hbm.at[:, lanes], sems.at[group])

    def one_part(part, near_ref, query_ref, local_ref, place_of):
        lanes = lanes_at(part)
        decay_ref[...] = jnp.exp(-rate_ref[:, lanes])
        decay = [spread(decay_ref[m : m + 1, :]) for m in range(poles)]
        reached = info_ref[REACHED, :]
        ahead = info_ref[AHEAD, :]
        carry = []
        for m in range(poles):
            entering = reached * jnp.exp(-before * spread(rate_ref[m : m + 1, lanes]))
            entering = entering * spread(incoming_ref[part, m : m + 1, :])
            entering = entering + local_ref[place_of, m * CHUNKS : (m + 1) * CHUNKS, :]
            carry.append(spread(gain_ref[m : m + 1, lanes]) * entering)
        for place in range(span):
            carry = [decay[m] * carry[m] for m in range(poles)]
            terms = list(carry)
            while len(terms) > 1:
                terms = [
                    terms[i] + terms[i + 1] if i + 1 < len(terms) else terms[i]
                    for i in range(0, len(terms), 2)
                ]
            carried = jnp.where(ahead > float(place), terms[0], 0.0)
            here = chunk_of(place)
            sx[pl.ds(place, CHUNKS, stride=span + 1), :] = (
                near_ref[place_of, here, :] + query_ref[place_of, here, :] * carried
            )
        for piece in range(CHUNKS):
            low = piece * (span + 1)
            stream = sx[low : low + span, :]
            native = slice(piece * span, (piece + 1) * span)
            stream_ref[native, lanes] = stream
            px[native, :] += stream * stream

    groups = stream_ref.shape[1] // GROUP
    sides = (
        (early, near_head, query_head, local_head),
        (0, near_a, query_a, local_a),
        (early + READY, near_b, query_b, local_b),
    )
    for first, near_ref, query_ref, local_ref in sides:

        @pl.loop(0, near_ref.shape[0] // inner)
        def _(group):
            if near_ref is near_a:
                for copy in fetch(group):
                    copy.wait()
            if near_ref is near_b:
                for copy in rest:
                    copy.wait()

            @pl.loop(group * inner, (group + 1) * inner)
            def _(part):
                one_part(part + first, near_ref, query_ref, local_ref, part)

            if near_ref is not near_b:
                copy_out(group + first // inner).start()

    for piece in range(rows // LANES):
        turned = px[piece * LANES : (piece + 1) * LANES, :].T
        power_ref[piece : piece + 1, :] = jnp.sum(turned, axis=0, keepdims=True)
    for group in range((early + READY) // inner):
        copy_out(group).wait()


def norm_kernel(width, left, power_ref, gain_ref, stream_ref, stream_in, out_hbm, stream_out, scale_ref, buffer, sems, left_sem):
    columns = pl.ds(left, stream_ref.shape[1] - left)
    rest = pltpu.make_async_copy(stream_ref.at[:, columns], stream_out.at[:, columns], left_sem.at[0])
    rest.start()
    scale = lax.rsqrt(jnp.sum(power_ref[...], axis=0) / width + 1e-06)
    for piece in range(scale.shape[0]):
        wide = jnp.broadcast_to(scale[piece : piece + 1, :], (LANES, LANES))
        scale_ref[piece * LANES : (piece + 1) * LANES, :] = wide.T
    rows = stream_ref.shape[0]
    count = sems.shape[0]
    tall = rows // count

    def copy_out(group):
        here = pl.ds(pl.multiple_of(group * tall, tall), tall)
        return pltpu.make_async_copy(buffer.at[here, :], out_hbm.at[here, :], sems.at[group])

    @pl.loop(0, count)
    def _(group):
        here = pl.ds(pl.multiple_of(group * tall, tall), tall)
        factor = scale_ref[here, :]
        for part in range(stream_ref.shape[1] // LANES):
            lanes = slice(part * LANES, (part + 1) * LANES)
            buffer[here, lanes] = stream_ref[here, lanes] * factor * gain_ref[:, lanes]
        copy_out(group).start()

    for group in range(count):
        copy_out(group).wait()
    rest.wait()


def shifted(block, axis, distance, wrap):
    count = lax.axis_size(axis)
    route = [(i, (i + distance) % count) for i in range(count) if wrap or i + distance < count]
    return lax.ppermute(block, axis, route)


def on_device(query_proj, key_proj, value_proj, short_filter, decay_rate, residue, skip_gain, norm_gain, residual, lengths):
    rows, width = query_proj.shape
    poles = decay_rate.shape[0]
    ranks = lax.axis_size("ctx")
    parts = width // LANES
    groups = width // GROUP
    near_by = pl.BlockSpec(memory_space=pltpu.VMEM)
    outside = pl.BlockSpec(memory_space=pltpu.HBM)
    limit = pltpu.CompilerParams(vmem_limit_bytes=12 * 1024 * 1024)
    shape = lambda *dims: jax.ShapeDtypeStruct(dims, F32)
    kept_near = lambda *dims: pltpu.VMEM(dims, F32)
    far_off = lambda array: pltpu.with_memory_space_constraint(array, pltpu.HBM)
    close_by = lambda array: pltpu.with_memory_space_constraint(array, pltpu.VMEM)
    query_proj, key_proj, value_proj, residual, short_filter, lengths = map(
        far_off, (query_proj, key_proj, value_proj, residual, short_filter, lengths)
    )

    rims = pl.pallas_call(
        rim_kernel,
        in_specs=[outside] * 3,
        out_specs=near_by,
        out_shape=pltpu.VMEM((3, 2, width), BF16),
        scratch_shapes=[pltpu.VMEM((3, 16, width), BF16), pltpu.SemaphoreType.DMA((3,))],
        name="rims",
    )(query_proj, key_proj, value_proj)
    rims = shifted(rims, "ctx", 1, False)
    pole_gain = residue * jnp.sqrt(-jnp.expm1(-2.0 * decay_rate))
    skip = skip_gain.reshape(1, width)

    early = FIRST_SHARE * (GROUP // LANES)
    late = parts - early
    pitch = rows + CHUNKS
    held = parts * poles // ranks
    k_here, v_here, q_a, r_a, taps_here, info = pl.pallas_call(
        functools.partial(fetch_kernel, rows),
        in_specs=[outside] * 6,
        out_specs=[near_by] * 6,
        out_shape=[
            pltpu.VMEM((rows, width), BF16),
            pltpu.VMEM((rows, width), BF16),
            pltpu.VMEM((rows, HEAD * LANES), BF16),
            pltpu.VMEM((rows, HEAD * LANES), BF16),
            kept_near(3, 3, width),
            kept_near(SECTIONS, LANES),
        ],
        scratch_shapes=[pltpu.SMEM(lengths.shape, jnp.int32), pltpu.SemaphoreType.DMA((6,))],
        compiler_params=limit,
        cost_estimate=pl.CostEstimate(flops=1000000, bytes_accessed=5000000, transcendentals=0),
        name="fetch",
    )(lengths, key_proj, value_proj, query_proj, residual, short_filter)
    info, k_here, v_here, taps_here = map(close_by, (info, k_here, v_here, taps_here))
    gated_a, gated_b, end, query_rim, query_taps = pl.pallas_call(
        functools.partial(end_kernel, rows, poles),
        in_specs=[near_by] * 6,
        out_specs=[near_by, outside, outside, near_by, near_by],
        out_shape=[
            kept_near(early, pitch, LANES),
            pltpu.HBM((late, pitch, LANES), F32),
            pltpu.HBM((parts, poles, LANES), F32),
            pltpu.VMEM((2, width), BF16),
            kept_near(3, width),
        ],
        scratch_shapes=[
            pltpu.VMEM((late, pitch, LANES), F32),
            pltpu.VMEM((parts, poles, LANES), F32),
            pltpu.VMEM((rows + 8, LANES), F32),
            pltpu.VMEM((rows + 8, LANES), F32),
            pltpu.VMEM((rows, LANES), F32),
            pltpu.VMEM((poles, LANES), F32),
            pltpu.SMEM((2, 8), jnp.int32),
            pltpu.SemaphoreType.DMA((late,)),
            pltpu.SemaphoreType.DMA((groups,)),
        ],
        compiler_params=limit,
        name="end_state",
    )(info, k_here, v_here, rims, taps_here, decay_rate)
    query_rim, query_taps = map(close_by, (query_rim, query_taps))

    pieces = lax.all_to_all(end.reshape(ranks, held, LANES), "ctx", 0, 0, tiled=True)

    def near_side(first, count, gated, q_part, r_part, early):
        block = (count, rows, LANES)
        states = (count, poles * CHUNKS, LANES)
        given = [info, query_rim, query_taps, decay_rate, pole_gain, skip, *map(close_by, (gated, q_part, r_part))]
        fetched = [query_proj, residual, far_off(gated_b)]
        scratch = [
            pltpu.VMEM((rows, count * LANES), BF16),
            pltpu.VMEM((rows, count * LANES), BF16),
            pltpu.VMEM((rows + 16, LANES), F32),
            pltpu.VMEM((rows + 16, LANES), F32),
            pltpu.VMEM((poles, LANES), F32),
            pltpu.SemaphoreType.DMA((3, 2)),
            pltpu.SemaphoreType.DMA((3, count)),
        ]
        if early:
            out_specs = [outside] * 3 + [near_by] * 4
            out_shape = [pltpu.HBM(dims, F32) for dims in (block, block, states)] + [
                kept_near(ranks, held, LANES),
                kept_near(HEAD, pitch, LANES),
                pltpu.VMEM((rows, HEAD * LANES), BF16),
                pltpu.VMEM((rows, HEAD * LANES), BF16),
            ]
            scratch = [pltpu.VMEM(dims, F32) for dims in (block, block, states)] + scratch
            scratch += [pltpu.SemaphoreType.DMA((3,))]
        else:
            out_specs = [near_by] * 3 + [outside] * 3
            out_shape = [kept_near(READY, *dims[1:]) for dims in (block, block, states)]
            out_shape += [pltpu.HBM((count - READY, *dims[1:]), F32) for dims in (block, block, states)]
            scratch = [pltpu.VMEM(dims, F32) for dims in ((count, pitch, LANES), block, block, states)] + scratch
        return pl.pallas_call(
            functools.partial(near_kernel, rows, poles, first, early),
            in_specs=[near_by] * len(given) + [outside] * len(fetched),
            out_specs=out_specs,
            out_shape=out_shape,
            scratch_shapes=scratch,
            compiler_params=limit,
            cost_estimate=pl.CostEstimate(flops=4000000, bytes_accessed=8000000, transcendentals=0),
            name="near",
        )(*given, *fetched)

    near_a, query_a, local_a, factors, gated_head, q_b, r_b = near_side(0, early, gated_a, q_a, r_a, True)
    near_b = near_side(early, late, gated_head, q_b, r_b, False)
    scanned = pl.pallas_call(
        scan_kernel,
        in_specs=[near_by, near_by],
        out_specs=outside,
        out_shape=pltpu.HBM((ranks, held, LANES), F32),
        scratch_shapes=[pltpu.VMEM((ranks, held, LANES), F32), pltpu.SemaphoreType.DMA((2,))],
        compiler_params=limit,
        name="rank_scan",
    )(close_by(factors), pieces)
    incoming = lax.all_to_all(scanned, "ctx", 0, 0, tiled=True).reshape(parts, poles, LANES)

    stream, kept, power = pl.pallas_call(
        functools.partial(stream_kernel, rows, poles),
        in_specs=[near_by] * 4 + [outside] * 3 + [near_by] * 3 + [outside] * 3,
        out_specs=[outside, near_by, near_by],
        out_shape=[pltpu.HBM((rows, width), F32), kept_near(rows, width), kept_near(rows // LANES, LANES)],
        scratch_shapes=[
            pltpu.VMEM((early, rows, LANES), F32),
            pltpu.VMEM((early, rows, LANES), F32),
            pltpu.VMEM((early, poles * CHUNKS, LANES), F32),
            pltpu.VMEM((late - READY, rows, LANES), F32),
            pltpu.VMEM((late - READY, rows, LANES), F32),
            pltpu.VMEM((late - READY, poles * CHUNKS, LANES), F32),
            pltpu.VMEM((rows + 8, LANES), F32),
            pltpu.VMEM((rows, LANES), F32),
            pltpu.VMEM((poles, LANES), F32),
            pltpu.SemaphoreType.DMA((groups,)),
            pltpu.SemaphoreType.DMA((3, early // (GROUP // LANES))),
            pltpu.SemaphoreType.DMA((3,)),
        ],
        compiler_params=limit,
        name="stream",
    )(
        info,
        decay_rate,
        pole_gain,
        incoming,
        *map(far_off, (near_a, query_a, local_a)),
        *map(close_by, near_b[:3]),
        *map(far_off, near_b[3:]),
    )
    shares = lax.axis_size("ch")
    near_first = sorted(range(1, shares), key=lambda hop: min(hop, shares - hop))
    powers = jnp.stack([power] + [shifted(power, "ch", hop, True) for hop in near_first])
    normed, stream = pl.pallas_call(
        functools.partial(norm_kernel, float(width * shares), (early + READY) * LANES),
        in_specs=[near_by, near_by, near_by, outside],
        out_specs=[outside, outside],
        out_shape=[pltpu.HBM((rows, width), F32)] * 2,
        input_output_aliases={3: 1},
        scratch_shapes=[
            pltpu.VMEM((rows, LANES), F32),
            pltpu.VMEM((rows, width), F32),
            pltpu.SemaphoreType.DMA((8,)),
            pltpu.SemaphoreType.DMA((1,)),
        ],
        compiler_params=limit,
        name="norm",
    )(powers, norm_gain.reshape(1, width), close_by(kept), far_off(stream))
    return (stream, normed)


def solution(mesh):
    placed = (
        P("ctx", "ch"),
        P("ctx", "ch"),
        P("ctx", "ch"),
        P(None, None, "ch"),
        P(None, "ch"),
        P(None, "ch"),
        P("ch"),
        P("ch"),
        P("ctx", "ch"),
        P(),
    )
    return jax.shard_map(
        on_device,
        mesh=mesh,
        in_specs=placed,
        out_specs=(P("ctx", "ch"), P("ctx", "ch")),
        check_vma=False,
    )
```

```python
import functools

import jax
import jax.numpy as jnp
from jax import lax
from jax.experimental import pallas as pl
from jax.experimental.pallas import tpu as pltpu
from jax.sharding import PartitionSpec as P

LANES = 128
CHUNKS = 8
GROUP = 256
FIRST_SHARE = 4
HEAD = 2
NEXT = 4
READY = 6
STEPS = 16
F32 = jnp.float32
BF16 = jnp.bfloat16


def starts_of(lengths_ref):
    first = lengths_ref[0]
    second = first + lengths_ref[1]
    third = second + lengths_ref[2]
    return (jnp.int32(0), first, second, third)


def spread(row):
    return jnp.broadcast_to(row, (CHUNKS, LANES))


def no_start(starts, where):
    kept = jnp.ones(where.shape, jnp.bool_)
    for start in starts:
        kept = kept & (where != start)
    return kept.astype(F32)


def any_in(starts, low, high):
    found = jnp.bool_(False)
    for start in starts:
        found = found | ((start >= low) & (start < high))
    return found


def block_has_start(starts, base, rows, block):
    found = jnp.bool_(False)
    for start in starts:
        inside = start - base
        place = lax.rem(jnp.maximum(inside, 0), rows // CHUNKS)
        found = found | (
            (inside >= 0) & (inside < rows) & (place >= block * STEPS) & (place < (block + 1) * STEPS)
        )
    return found


def lanes_at(part):
    return pl.ds(pl.multiple_of(part * LANES, LANES), LANES)


def chunk_of(place):
    return pl.ds(pl.multiple_of(place * CHUNKS, CHUNKS), CHUNKS)


def lay_out(source, lanes, target, span, offset):
    for piece in range(CHUNKS):
        low = offset + piece * (span + 1)
        target[low : low + span, :] = source[piece * span : (piece + 1) * span, lanes].astype(F32)


def rim_kernel(q_hbm, k_hbm, v_hbm, out_ref, buffer, sems):
    tail = buffer.shape[1]
    copies = [
        pltpu.make_async_copy(source.at[pl.ds(source.shape[0] - tail, tail), :], buffer.at[i], sems.at[i])
        for i, source in enumerate((q_hbm, k_hbm, v_hbm))
    ]
    for copy in copies:
        copy.start()
    for i, copy in enumerate(copies):
        copy.wait()
        out_ref[i] = buffer[i, tail - 2 :, :]


def walk(span, flags, run, carry):
    for block in range(span // STEPS):
        carry = lax.cond(
            flags[block], functools.partial(run, block, True), functools.partial(run, block, False), carry
        )
    return carry


SEGMENTS = 4
FAR, JOINED, REACHED, AHEAD, FLAGS, BEGUN, INSIDE = (slice(i * CHUNKS, (i + 1) * CHUNKS) for i in (0, 1, 2, 3, 4, 5, 5 + SEGMENTS))
SECTIONS = (5 + 2 * SEGMENTS) * CHUNKS


def describe(starts, base, rows, info_ref):
    span = rows // CHUNKS
    chunk = lax.broadcasted_iota(jnp.int32, (CHUNKS, LANES), 0)
    chunk_row = base + chunk * span
    alive = jnp.ones((CHUNKS, LANES), jnp.bool_)
    reached = jnp.ones((CHUNKS, LANES), jnp.bool_)
    ahead = jnp.full((CHUNKS, LANES), span, jnp.int32)
    for start in starts:
        inside = start - chunk_row
        alive = alive & ((inside < 0) | (inside >= span))
        reached = reached & ((start < base) | (inside >= 0))
        ahead = jnp.where((inside >= 0) & (inside < ahead), inside, ahead)
    info_ref[FAR, :] = no_start(starts, chunk_row - 1)
    info_ref[JOINED, :] = (alive & (chunk > 0)).astype(F32)
    info_ref[REACHED, :] = reached.astype(F32)
    info_ref[AHEAD, :] = ahead.astype(F32)
    for block in range(span // STEPS):
        flag = jnp.where(block_has_start(starts, base, rows, block), 1.0, 0.0)
        info_ref[FLAGS.start + block : FLAGS.start + block + 1, :] = jnp.full((1, LANES), flag, F32)
    for i, start in enumerate(starts):
        rank = lax.div(start, rows).astype(F32)
        low = BEGUN.start + i * CHUNKS
        info_ref[low : low + CHUNKS, :] = jnp.full((CHUNKS, LANES), rank, F32)
        low = INSIDE.start + i * CHUNKS
        info_ref[low : low + CHUNKS, :] = (start - chunk_row).astype(F32)


def pitched(row, span):
    return row + lax.div(row, span)


def fetch_kernel(rows, lengths_hbm, k_hbm, v_hbm, q_hbm, res_hbm, taps_hbm, k_ref, v_ref, q_next, r_next, taps_ref, info_ref, lengths_ref, sems):
    columns = pl.ds(0, q_next.shape[1])
    pairs = (
        (lengths_hbm, lengths_ref),
        (k_hbm, k_ref),
        (v_hbm, v_ref),
        (q_hbm.at[:, columns], q_next),
        (res_hbm.at[:, columns], r_next),
        (taps_hbm, taps_ref),
    )
    copies = [pltpu.make_async_copy(source, target, sems.at[i]) for i, (source, target) in enumerate(pairs)]
    for copy in copies:
        copy.start()
    copies[0].wait()
    describe(starts_of(lengths_ref), lax.axis_index("ctx") * rows, rows, info_ref)
    for copy in copies[1:]:
        copy.wait()


def end_kernel(rows, poles, info_ref, k_ref, v_ref, rim_ref, taps_ref, rate_ref, gated_a, gated_hbm, end_hbm, rim_next, taps_next, gated_b, end_ref, kx, vx, gx, decay_ref, mends, out_sems, end_sems):
    span = rows // CHUNKS
    phase = lax.broadcasted_iota(jnp.int32, (CHUNKS, LANES), 0)
    groups = k_ref.shape[1] // GROUP
    rim_next[...] = rim_ref[0]
    taps_next[...] = taps_ref[0]
    last = jnp.int32(0)
    mended = jnp.int32(0)
    for i in range(SEGMENTS):
        low = INSIDE.start + i * CHUNKS
        inside = jnp.max(info_ref[low : low + 1, :]).astype(jnp.int32)
        here_now = (inside >= 0) & (inside < rows)
        last = jnp.where(here_now, inside, last)
        for row, reach, wanted in (
            (inside, 0, here_now),
            (inside + 1, 1, (inside >= -1) & (inside < rows - 1)),
        ):
            mends[0, mended] = jnp.where(wanted, row, 0)
            mends[1, mended] = reach
            mended = mended + wanted.astype(jnp.int32)
    inner = GROUP // LANES

    def store(here):
        return pltpu.make_async_copy(gated_b.at[here], gated_hbm.at[here], out_sems.at[here])

    def send(group):
        here = pl.ds(group * inner, inner)
        return pltpu.make_async_copy(end_ref.at[here], end_hbm.at[here], end_sems.at[group])

    def one_group(group, first, gated_ref):
        @pl.loop(group * inner, (group + 1) * inner)
        def _(part):
            lanes = lanes_at(part)
            here = part - first * inner
            for i, source, target in ((1, k_ref, kx), (2, v_ref, vx)):
                target[6:8, :] = rim_ref[i, :, lanes].astype(F32)
                target[8:, :] = source[:, lanes].astype(F32)
            decay_ref[...] = jnp.exp(-float(CHUNKS) * rate_ref[:, lanes])
            lines = [[taps_ref[i, j : j + 1, lanes] for j in range(3)] for i in (1, 2)]
            taps = [[spread(line) for line in three] for three in lines]
            for block in range(rows // CHUNKS):
                low = block * CHUNKS
                shorts = []
                for three, source in zip(taps, (kx, vx)):
                    short = three[0] * source[low + 8 : low + 16, :]
                    for back in (1, 2):
                        short = short + three[back] * source[low + 8 - back : low + 16 - back, :]
                    shorts.append(short)
                gated = shorts[0] * shorts[1]
                gx[low : low + CHUNKS, :] = gated
                to = low + low // span
                gated_ref[here, to : to + CHUNKS, :] = gated

            @pl.when(mended > 0)
            def _():
                @pl.loop(0, mended)
                def _(i):
                    row = mends[0, i]
                    reach = mends[1, i].astype(F32)
                    shorts = []
                    for three, source in zip(lines, (kx, vx)):
                        now = three[0] * source[pl.ds(row + 8, 1), :]
                        shorts.append(now + three[1] * source[pl.ds(row + 7, 1), :] * reach)
                    gated = shorts[0] * shorts[1]
                    gx[pl.ds(row, 1), :] = gated
                    gated_ref[here, pl.ds(pitched(row, span), 1), :] = gated

                for block in range(rows // CHUNKS):
                    low = block * CHUNKS
                    gx[low : low + CHUNKS, :] = jnp.where(
                        phase + low >= last, gx[low : low + CHUNKS, :], 0.0
                    )

            decay = [spread(decay_ref[m : m + 1, :]) for m in range(poles)]
            sums = [gx[:CHUNKS, :] for _ in range(poles)]
            for block in range(1, rows // CHUNKS):
                gated = gx[block * CHUNKS : (block + 1) * CHUNKS, :]
                sums = [decay[m] * sums[m] + gated for m in range(poles)]
            after = (phase - (CHUNKS - 1)).astype(F32)
            for m in range(poles):
                weight = jnp.exp(after * spread(rate_ref[m : m + 1, lanes]))
                end_ref[part, m : m + 1, :] = jnp.sum(weight * sums[m], axis=0, keepdims=True)
            if first:
                store(here).start()

        send(group).start()

    middle = gated_a.shape[0] // inner
    pl.loop(middle, groups)(lambda group: one_group(group, middle, gated_b))
    pl.loop(0, middle)(lambda group: one_group(group, 0, gated_a))
    for here in range(gated_b.shape[0]):
        store(here).wait()
    for group in range(groups):
        send(group).wait()


def rank_factors(info_ref, rows, poles, rate_ref, out_ref):
    ranks, held = out_ref.shape[:2]
    shares = poles // held
    mine = lax.axis_index("ctx")
    lanes = lanes_at(lax.div(mine, shares))
    rate = rate_ref[:held, lanes]
    for share in range(1, shares):
        theirs = rate_ref[share * held : (share + 1) * held, lanes]
        rate = jnp.where(lax.rem(mine, shares) == share, theirs, rate)
    whole = jnp.exp(-float(rows) * rate)
    begun = [info_ref[BEGUN.start + i * CHUNKS : BEGUN.start + i * CHUNKS + held, :] for i in range(1, SEGMENTS)]
    for rank in range(ranks):
        kept = whole
        for begin in begun:
            kept = jnp.where(begin == float(rank), 0.0, kept)
        out_ref[rank] = kept


def scan_kernel(factor_ref, pieces_ref, out_hbm, out_ref, sems):
    running = jnp.zeros(pieces_ref.shape[1:], F32)
    ranks = pieces_ref.shape[0]
    block = ranks // sems.shape[0]
    copies = []
    for rank in range(ranks):
        out_ref[rank] = running
        running = factor_ref[rank] * running + pieces_ref[rank]
        if rank % block == block - 1:
            here = pl.ds(rank - block + 1, block)
            copies.append(pltpu.make_async_copy(out_ref.at[here], out_hbm.at[here], sems.at[rank // block]))
            copies[-1].start()
    for copy in copies:
        copy.wait()


def near_kernel(rows, poles, first, early, info_ref, rim_ref, taps_ref, rate_ref, gain_ref, skip_ref, gated_in, q_in, r_in, q_hbm, res_hbm, gated_hbm, *others):
    if early:
        outs, (factor_ref, gated_next, q_next, r_next, *others) = others[:3], others[3:]
        near_ref, query_ref, local_ref, q_ref, r_ref, qx, rx, decay_ref, own_sems, far_sems, next_sems = others
        gated_ref = gated_in
        count = near_ref.shape[0]
    else:
        heads, tails, others = others[:3], others[3:6], others[6:]
        gated_ref, near_ref, query_ref, local_ref, q_ref, r_ref, qx, rx, decay_ref, own_sems, far_sems = others
        count = near_ref.shape[0]

    cuts = ((HEAD, NEXT), (NEXT, count))

    def fetch(cut):
        low, high = cuts[cut]
        from_columns = pl.ds((first + low) * LANES, (high - low) * LANES)
        columns = pl.ds(low * LANES, (high - low) * LANES)
        pairs = [(source.at[:, from_columns], target.at[:, columns]) for source, target in ((q_hbm, q_ref), (res_hbm, r_ref))]
        if not early:
            blocks = pl.ds(low, high - low)
            pairs.append((gated_hbm.at[blocks], gated_ref.at[blocks]))
        return [
            pltpu.make_async_copy(source, target, own_sems.at[i, cut])
            for i, (source, target) in enumerate(pairs)
        ]

    for cut in range(len(cuts)):
        for copy in fetch(cut):
            copy.start()
    for i, (source, target) in enumerate(((q_in, q_ref), (r_in, r_ref))):
        target[:, : HEAD * LANES] = source[...]
    if early:
        columns = pl.ds((first + count) * LANES, HEAD * LANES)
        pairs = (
            (gated_hbm.at[pl.ds(0, HEAD)], gated_next),
            (q_hbm.at[:, columns], q_next),
            (res_hbm.at[:, columns], r_next),
        )
        ahead_of_time = [
            pltpu.make_async_copy(source, target, next_sems.at[i]) for i, (source, target) in enumerate(pairs)
        ]
        for copy in ahead_of_time:
            copy.start()
        rank_factors(info_ref, rows, poles, rate_ref, factor_ref)
    else:
        gated_ref[:HEAD] = gated_in[...]
    span = rows // CHUNKS
    chunk = lax.broadcasted_iota(jnp.int32, (CHUNKS, LANES), 0)
    flags = [
        jnp.max(info_ref[FLAGS.start + block : FLAGS.start + block + 1, :]) > 0.0
        for block in range(span // STEPS)
    ]

    made = (near_ref, query_ref, local_ref)

    def store(here, targets, low):
        return [
            pltpu.make_async_copy(source.at[here], target.at[here - low], far_sems.at[i, here])
            for i, (source, target) in enumerate(zip(made, targets))
        ]

    @pl.loop(0, count)
    def _(here):
        own = lanes_at(here)
        lanes = lanes_at(here + first)
        far = info_ref[FAR, :]
        joined = info_ref[JOINED, :]

        for cut, (low, _) in enumerate(cuts):

            @pl.when(here == low)
            def _():
                for copy in fetch(cut):
                    copy.wait()

        qx[5:7, :] = rim_ref[:, lanes].astype(F32)
        lay_out(q_ref, own, qx, span, 8)
        lay_out(r_ref, own, rx, span, 0)
        decay_ref[...] = jnp.exp(-rate_ref[:, lanes])
        taps = [spread(taps_ref[j : j + 1, lanes]) for j in range(3)]
        skip = spread(skip_ref[:, lanes])
        decay = [spread(decay_ref[m : m + 1, :]) for m in range(poles)]
        gain = [spread(gain_ref[m : m + 1, lanes]) for m in range(poles)]
        carry = [
            qx[pl.ds(6, CHUNKS, stride=span + 1), :],
            qx[pl.ds(5, CHUNKS, stride=span + 1), :] * far,
        ] + [jnp.zeros((CHUNKS, LANES), F32)] * poles

        def run(block, masked, carry):
            carry = list(carry)
            for step in range(STEPS):
                place = block * STEPS + step
                if masked:
                    keep = jnp.ones((CHUNKS, LANES), F32)
                    for i in range(SEGMENTS):
                        low = INSIDE.start + i * CHUNKS
                        keep = jnp.where(info_ref[low : low + CHUNKS, :] == float(place), 0.0, keep)
                    carry = [held * keep for held in carry]
                query = qx[pl.ds(8 + place, CHUNKS, stride=span + 1), :]
                query_short = taps[0] * query + taps[1] * carry[0] + taps[2] * carry[1]
                gated = gated_ref[here, pl.ds(place, CHUNKS, stride=span + 1), :]
                states = [decay[m] * carry[2 + m] + gated for m in range(poles)]
                total = skip * gated
                for m in range(poles):
                    total = total + gain[m] * states[m]
                query_ref[here, chunk_of(place), :] = query_short
                near_ref[here, chunk_of(place), :] = (
                    rx[pl.ds(place, CHUNKS, stride=span + 1), :] + query_short * total
                )
                carry = [query, carry[0]] + states
            return tuple(carry)

        carry = walk(span, flags, run, tuple(carry))
        for m in range(poles):
            reach = jnp.exp(-float(span) * spread(rate_ref[m : m + 1, lanes])) * joined
            state = carry[2 + m]
            for hop in (1, 2, 4):
                state = state + reach * pltpu.roll(state, hop, 0)
                if hop < 4:
                    reach = reach * pltpu.roll(reach, hop, 0)
            local_ref[here, m * CHUNKS : (m + 1) * CHUNKS, :] = jnp.where(
                chunk > 0, pltpu.roll(state, 1, 0), 0.0
            )
        if early:
            for copy in store(here, outs, 0):
                copy.start()
        else:

            @pl.when(here < READY)
            def _():
                for source, target in zip(made, heads):
                    target[here] = source[here]

            @pl.when(here >= READY)
            def _():
                for copy in store(here, tails, READY):
                    copy.start()

    if early:
        for copy in ahead_of_time:
            copy.wait()
    for here in range(0 if early else READY, count):
        for copy in store(here, outs, 0) if early else store(here, tails, READY):
            copy.wait()


def stream_kernel(rows, poles, info_ref, rate_ref, gain_ref, incoming_ref, near_hbm, query_hbm, local_hbm, near_head, query_head, local_head, near_rest, query_rest, local_rest, out_hbm, stream_ref, power_ref, near_a, query_a, local_a, near_b, query_b, local_b, sx, px, decay_ref, sems, far_sems, rest_sems):
    span = rows // CHUNKS
    chunk = lax.broadcasted_iota(jnp.int32, (CHUNKS, LANES), 0)
    px[...] = jnp.zeros_like(px)
    inner = GROUP // LANES
    early = near_a.shape[0]

    def fetch(group):
        here = pl.ds(group * inner, inner)
        pairs = ((near_hbm, near_a), (query_hbm, query_a), (local_hbm, local_a))
        return [
            pltpu.make_async_copy(source.at[here], target.at[here], far_sems.at[i, group])
            for i, (source, target) in enumerate(pairs)
        ]

    pairs = ((near_rest, near_b), (query_rest, query_b), (local_rest, local_b))
    rest = [pltpu.make_async_copy(source, target, rest_sems.at[i]) for i, (source, target) in enumerate(pairs)]
    for group in range(early // inner):
        for copy in fetch(group):
            copy.start()
    for copy in rest:
        copy.start()
    before = (chunk * span).astype(F32)

    def copy_out(group):
        lanes = pl.ds(pl.multiple_of(group * GROUP, GROUP), GROUP)
        return pltpu.make_async_copy(stream_ref.at[:, lanes], out_hbm.at[:, lanes], sems.at[group])

    def one_part(part, near_ref, query_ref, local_ref, place_of):
        lanes = lanes_at(part)
        decay_ref[...] = jnp.exp(-rate_ref[:, lanes])
        decay = [spread(decay_ref[m : m + 1, :]) for m in range(poles)]
        reached = info_ref[REACHED, :]
        ahead = info_ref[AHEAD, :]
        carry = []
        for m in range(poles):
            entering = reached * jnp.exp(-before * spread(rate_ref[m : m + 1, lanes]))
            entering = entering * spread(incoming_ref[part, m : m + 1, :])
            entering = entering + local_ref[place_of, m * CHUNKS : (m + 1) * CHUNKS, :]
            carry.append(spread(gain_ref[m : m + 1, lanes]) * entering)
        for place in range(span):
            carry = [decay[m] * carry[m] for m in range(poles)]
            terms = list(carry)
            while len(terms) > 1:
                terms = [
                    terms[i] + terms[i + 1] if i + 1 < len(terms) else terms[i]
                    for i in range(0, len(terms), 2)
                ]
            carried = jnp.where(ahead > float(place), terms[0], 0.0)
            here = chunk_of(place)
            sx[pl.ds(place, CHUNKS, stride=span + 1), :] = (
                near_ref[place_of, here, :] + query_ref[place_of, here, :] * carried
            )
        for piece in range(CHUNKS):
            low = piece * (span + 1)
            stream = sx[low : low + span, :]
            native = slice(piece * span, (piece + 1) * span)
            stream_ref[native, lanes] = stream
            px[native, :] += stream * stream

    groups = stream_ref.shape[1] // GROUP
    sides = (
        (early, near_head, query_head, local_head),
        (0, near_a, query_a, local_a),
        (early + READY, near_b, query_b, local_b),
    )
    for first, near_ref, query_ref, local_ref in sides:

        @pl.loop(0, near_ref.shape[0] // inner)
        def _(group):
            if near_ref is near_a:
                for copy in fetch(group):
                    copy.wait()
            if near_ref is near_b:
                for copy in rest:
                    copy.wait()

            @pl.loop(group * inner, (group + 1) * inner)
            def _(part):
                one_part(part + first, near_ref, query_ref, local_ref, part)

            if near_ref is not near_b:
                copy_out(group + first // inner).start()

    for piece in range(rows // LANES):
        turned = px[piece * LANES : (piece + 1) * LANES, :].T
        power_ref[piece : piece + 1, :] = jnp.sum(turned, axis=0, keepdims=True)
    for group in range((early + READY) // inner):
        copy_out(group).wait()


def norm_kernel(width, left, power_ref, gain_ref, stream_ref, stream_in, out_hbm, stream_out, scale_ref, buffer, sems, left_sem):
    columns = pl.ds(left, stream_ref.shape[1] - left)
    rest = pltpu.make_async_copy(stream_ref.at[:, columns], stream_out.at[:, columns], left_sem.at[0])
    rest.start()
    scale = lax.rsqrt(jnp.sum(power_ref[...], axis=0) / width + 1e-06)
    for piece in range(scale.shape[0]):
        wide = jnp.broadcast_to(scale[piece : piece + 1, :], (LANES, LANES))
        scale_ref[piece * LANES : (piece + 1) * LANES, :] = wide.T
    rows = stream_ref.shape[0]
    count = sems.shape[0]
    tall = rows // count

    def copy_out(group):
        here = pl.ds(pl.multiple_of(group * tall, tall), tall)
        return pltpu.make_async_copy(buffer.at[here, :], out_hbm.at[here, :], sems.at[group])

    @pl.loop(0, count)
    def _(group):
        here = pl.ds(pl.multiple_of(group * tall, tall), tall)
        factor = scale_ref[here, :]
        for part in range(stream_ref.shape[1] // LANES):
            lanes = slice(part * LANES, (part + 1) * LANES)
            buffer[here, lanes] = stream_ref[here, lanes] * factor * gain_ref[:, lanes]
        copy_out(group).start()

    for group in range(count):
        copy_out(group).wait()
    rest.wait()


def shifted(block, axis, distance):
    count = lax.axis_size(axis)
    return lax.ppermute(block, axis, [(i, (i + distance) % count) for i in range(count)])


def on_device(query_proj, key_proj, value_proj, short_filter, decay_rate, residue, skip_gain, norm_gain, residual, lengths):
    rows, width = query_proj.shape
    poles = decay_rate.shape[0]
    ranks = lax.axis_size("ctx")
    parts = width // LANES
    groups = width // GROUP
    near_by = pl.BlockSpec(memory_space=pltpu.VMEM)
    outside = pl.BlockSpec(memory_space=pltpu.HBM)
    limit = pltpu.CompilerParams(vmem_limit_bytes=12 * 1024 * 1024)
    shape = lambda *dims: jax.ShapeDtypeStruct(dims, F32)
    kept_near = lambda *dims: pltpu.VMEM(dims, F32)
    far_off = lambda array: pltpu.with_memory_space_constraint(array, pltpu.HBM)
    close_by = lambda array: pltpu.with_memory_space_constraint(array, pltpu.VMEM)
    query_proj, key_proj, value_proj, residual, short_filter, lengths = map(
        far_off, (query_proj, key_proj, value_proj, residual, short_filter, lengths)
    )

    rims = pl.pallas_call(
        rim_kernel,
        in_specs=[outside] * 3,
        out_specs=near_by,
        out_shape=pltpu.VMEM((3, 2, width), BF16),
        scratch_shapes=[pltpu.VMEM((3, 16, width), BF16), pltpu.SemaphoreType.DMA((3,))],
        name="rims",
    )(query_proj, key_proj, value_proj)
    rims = shifted(rims, "ctx", 1)
    pole_gain = residue * jnp.sqrt(-jnp.expm1(-2.0 * decay_rate))
    skip = skip_gain.reshape(1, width)

    early = FIRST_SHARE * (GROUP // LANES)
    late = parts - early
    pitch = rows + CHUNKS
    held = parts * poles // ranks
    k_here, v_here, q_a, r_a, taps_here, info = pl.pallas_call(
        functools.partial(fetch_kernel, rows),
        in_specs=[outside] * 6,
        out_specs=[near_by] * 6,
        out_shape=[
            pltpu.VMEM((rows, width), BF16),
            pltpu.VMEM((rows, width), BF16),
            pltpu.VMEM((rows, HEAD * LANES), BF16),
            pltpu.VMEM((rows, HEAD * LANES), BF16),
            kept_near(3, 3, width),
            kept_near(SECTIONS, LANES),
        ],
        scratch_shapes=[pltpu.SMEM(lengths.shape, jnp.int32), pltpu.SemaphoreType.DMA((6,))],
        compiler_params=limit,
        cost_estimate=pl.CostEstimate(flops=1000000, bytes_accessed=5000000, transcendentals=0),
        name="fetch",
    )(lengths, key_proj, value_proj, query_proj, residual, short_filter)
    info, k_here, v_here, taps_here = map(close_by, (info, k_here, v_here, taps_here))
    gated_a, gated_b, end, query_rim, query_taps = pl.pallas_call(
        functools.partial(end_kernel, rows, poles),
        in_specs=[near_by] * 6,
        out_specs=[near_by, outside, outside, near_by, near_by],
        out_shape=[
            kept_near(early, pitch, LANES),
            pltpu.HBM((late, pitch, LANES), F32),
            pltpu.HBM((parts, poles, LANES), F32),
            pltpu.VMEM((2, width), BF16),
            kept_near(3, width),
        ],
        scratch_shapes=[
            pltpu.VMEM((late, pitch, LANES), F32),
            pltpu.VMEM((parts, poles, LANES), F32),
            pltpu.VMEM((rows + 8, LANES), F32),
            pltpu.VMEM((rows + 8, LANES), F32),
            pltpu.VMEM((rows, LANES), F32),
            pltpu.VMEM((poles, LANES), F32),
            pltpu.SMEM((2, 8), jnp.int32),
            pltpu.SemaphoreType.DMA((late,)),
            pltpu.SemaphoreType.DMA((groups,)),
        ],
        compiler_params=limit,
        name="end_state",
    )(info, k_here, v_here, rims, taps_here, decay_rate)
    query_rim, query_taps = map(close_by, (query_rim, query_taps))

    pieces = lax.all_to_all(end.reshape(ranks, held, LANES), "ctx", 0, 0, tiled=True)

    def near_side(first, count, gated, q_part, r_part, early):
        block = (count, rows, LANES)
        states = (count, poles * CHUNKS, LANES)
        given = [info, query_rim, query_taps, decay_rate, pole_gain, skip, *map(close_by, (gated, q_part, r_part))]
        fetched = [query_proj, residual, far_off(gated_b)]
        scratch = [
            pltpu.VMEM((rows, count * LANES), BF16),
            pltpu.VMEM((rows, count * LANES), BF16),
            pltpu.VMEM((rows + 16, LANES), F32),
            pltpu.VMEM((rows + 16, LANES), F32),
            pltpu.VMEM((poles, LANES), F32),
            pltpu.SemaphoreType.DMA((3, 2)),
            pltpu.SemaphoreType.DMA((3, count)),
        ]
        if early:
            out_specs = [outside] * 3 + [near_by] * 4
            out_shape = [pltpu.HBM(dims, F32) for dims in (block, block, states)] + [
                kept_near(ranks, held, LANES),
                kept_near(HEAD, pitch, LANES),
                pltpu.VMEM((rows, HEAD * LANES), BF16),
                pltpu.VMEM((rows, HEAD * LANES), BF16),
            ]
            scratch = [pltpu.VMEM(dims, F32) for dims in (block, block, states)] + scratch
            scratch += [pltpu.SemaphoreType.DMA((3,))]
        else:
            out_specs = [near_by] * 3 + [outside] * 3
            out_shape = [kept_near(READY, *dims[1:]) for dims in (block, block, states)]
            out_shape += [pltpu.HBM((count - READY, *dims[1:]), F32) for dims in (block, block, states)]
            scratch = [pltpu.VMEM(dims, F32) for dims in ((count, pitch, LANES), block, block, states)] + scratch
        return pl.pallas_call(
            functools.partial(near_kernel, rows, poles, first, early),
            in_specs=[near_by] * len(given) + [outside] * len(fetched),
            out_specs=out_specs,
            out_shape=out_shape,
            scratch_shapes=scratch,
            compiler_params=limit,
            cost_estimate=pl.CostEstimate(flops=4000000, bytes_accessed=8000000, transcendentals=0),
            name="near",
        )(*given, *fetched)

    near_a, query_a, local_a, factors, gated_head, q_b, r_b = near_side(0, early, gated_a, q_a, r_a, True)
    near_b = near_side(early, late, gated_head, q_b, r_b, False)
    scanned = pl.pallas_call(
        scan_kernel,
        in_specs=[near_by, near_by],
        out_specs=outside,
        out_shape=pltpu.HBM((ranks, held, LANES), F32),
        scratch_shapes=[pltpu.VMEM((ranks, held, LANES), F32), pltpu.SemaphoreType.DMA((2,))],
        compiler_params=limit,
        name="rank_scan",
    )(close_by(factors), pieces)
    incoming = lax.all_to_all(scanned, "ctx", 0, 0, tiled=True).reshape(parts, poles, LANES)

    stream, kept, power = pl.pallas_call(
        functools.partial(stream_kernel, rows, poles),
        in_specs=[near_by] * 4 + [outside] * 3 + [near_by] * 3 + [outside] * 3,
        out_specs=[outside, near_by, near_by],
        out_shape=[pltpu.HBM((rows, width), F32), kept_near(rows, width), kept_near(rows // LANES, LANES)],
        scratch_shapes=[
            pltpu.VMEM((early, rows, LANES), F32),
            pltpu.VMEM((early, rows, LANES), F32),
            pltpu.VMEM((early, poles * CHUNKS, LANES), F32),
            pltpu.VMEM((late - READY, rows, LANES), F32),
            pltpu.VMEM((late - READY, rows, LANES), F32),
            pltpu.VMEM((late - READY, poles * CHUNKS, LANES), F32),
            pltpu.VMEM((rows + 8, LANES), F32),
            pltpu.VMEM((rows, LANES), F32),
            pltpu.VMEM((poles, LANES), F32),
            pltpu.SemaphoreType.DMA((groups,)),
            pltpu.SemaphoreType.DMA((3, early // (GROUP // LANES))),
            pltpu.SemaphoreType.DMA((3,)),
        ],
        compiler_params=limit,
        name="stream",
    )(
        info,
        decay_rate,
        pole_gain,
        incoming,
        *map(far_off, (near_a, query_a, local_a)),
        *map(close_by, near_b[:3]),
        *map(far_off, near_b[3:]),
    )
    shares = lax.axis_size("ch")
    near_first = sorted(range(1, shares), key=lambda hop: min(hop, shares - hop))
    powers = jnp.stack([power] + [shifted(power, "ch", hop) for hop in near_first])
    normed, stream = pl.pallas_call(
        functools.partial(norm_kernel, float(width * shares), (early + READY) * LANES),
        in_specs=[near_by, near_by, near_by, outside],
        out_specs=[outside, outside],
        out_shape=[pltpu.HBM((rows, width), F32)] * 2,
        input_output_aliases={3: 1},
        scratch_shapes=[
            pltpu.VMEM((rows, LANES), F32),
            pltpu.VMEM((rows, width), F32),
            pltpu.SemaphoreType.DMA((8,)),
            pltpu.SemaphoreType.DMA((1,)),
        ],
        compiler_params=limit,
        name="norm",
    )(powers, norm_gain.reshape(1, width), close_by(kept), far_off(stream))
    return (stream, normed)


def solution(mesh):
    placed = (
        P("ctx", "ch"),
        P("ctx", "ch"),
        P("ctx", "ch"),
        P(None, None, "ch"),
        P(None, "ch"),
        P(None, "ch"),
        P("ch"),
        P("ch"),
        P("ctx", "ch"),
        P(),
    )
    return jax.shard_map(
        on_device,
        mesh=mesh,
        in_specs=placed,
        out_specs=(P("ctx", "ch"), P("ctx", "ch")),
        check_vma=False,
    )
```

```python
import functools

import jax
import jax.numpy as jnp
from jax import lax
from jax.experimental import pallas as pl
from jax.experimental.pallas import tpu as pltpu
from jax.sharding import PartitionSpec as P

LANES = 128
CHUNKS = 8
GROUP = 256
FIRST_SHARE = 4
HEAD = 2
NEXT = 4
READY = 6
STEPS = 16
F32 = jnp.float32
BF16 = jnp.bfloat16


def starts_of(lengths_ref):
    first = lengths_ref[0]
    second = first + lengths_ref[1]
    third = second + lengths_ref[2]
    return (jnp.int32(0), first, second, third)


def spread(row):
    return jnp.broadcast_to(row, (CHUNKS, LANES))


def no_start(starts, where):
    kept = jnp.ones(where.shape, jnp.bool_)
    for start in starts:
        kept = kept & (where != start)
    return kept.astype(F32)


def any_in(starts, low, high):
    found = jnp.bool_(False)
    for start in starts:
        found = found | ((start >= low) & (start < high))
    return found


def block_has_start(starts, base, rows, block):
    found = jnp.bool_(False)
    for start in starts:
        inside = start - base
        place = lax.rem(jnp.maximum(inside, 0), rows // CHUNKS)
        found = found | (
            (inside >= 0) & (inside < rows) & (place >= block * STEPS) & (place < (block + 1) * STEPS)
        )
    return found


def lanes_at(part):
    return pl.ds(pl.multiple_of(part * LANES, LANES), LANES)


def chunk_of(place):
    return pl.ds(pl.multiple_of(place * CHUNKS, CHUNKS), CHUNKS)


def lay_out(source, lanes, target, span, offset):
    for piece in range(CHUNKS):
        low = offset + piece * (span + 1)
        target[low : low + span, :] = source[piece * span : (piece + 1) * span, lanes].astype(F32)


def rim_kernel(q_hbm, k_hbm, v_hbm, out_ref, buffer, sems):
    tail = buffer.shape[1]
    copies = [
        pltpu.make_async_copy(source.at[pl.ds(source.shape[0] - tail, tail), :], buffer.at[i], sems.at[i])
        for i, source in enumerate((q_hbm, k_hbm, v_hbm))
    ]
    for copy in copies:
        copy.start()
    for i, copy in enumerate(copies):
        copy.wait()
        out_ref[i] = buffer[i, tail - 2 :, :]


def walk(span, flags, run, carry):
    for block in range(span // STEPS):
        carry = lax.cond(
            flags[block], functools.partial(run, block, True), functools.partial(run, block, False), carry
        )
    return carry


SEGMENTS = 4
FAR, JOINED, REACHED, AHEAD, FLAGS, BEGUN, INSIDE = (slice(i * CHUNKS, (i + 1) * CHUNKS) for i in (0, 1, 2, 3, 4, 5, 5 + SEGMENTS))
SECTIONS = (5 + 2 * SEGMENTS) * CHUNKS


def describe(starts, base, rows, info_ref):
    span = rows // CHUNKS
    chunk = lax.broadcasted_iota(jnp.int32, (CHUNKS, LANES), 0)
    chunk_row = base + chunk * span
    alive = jnp.ones((CHUNKS, LANES), jnp.bool_)
    reached = jnp.ones((CHUNKS, LANES), jnp.bool_)
    ahead = jnp.full((CHUNKS, LANES), span, jnp.int32)
    for start in starts:
        inside = start - chunk_row
        alive = alive & ((inside < 0) | (inside >= span))
        reached = reached & ((start < base) | (inside >= 0))
        ahead = jnp.where((inside >= 0) & (inside < ahead), inside, ahead)
    info_ref[FAR, :] = no_start(starts, chunk_row - 1)
    info_ref[JOINED, :] = (alive & (chunk > 0)).astype(F32)
    info_ref[REACHED, :] = reached.astype(F32)
    info_ref[AHEAD, :] = ahead.astype(F32)
    for block in range(span // STEPS):
        flag = jnp.where(block_has_start(starts, base, rows, block), 1.0, 0.0)
        info_ref[FLAGS.start + block : FLAGS.start + block + 1, :] = jnp.full((1, LANES), flag, F32)
    for i, start in enumerate(starts):
        rank = lax.div(start, rows).astype(F32)
        low = BEGUN.start + i * CHUNKS
        info_ref[low : low + CHUNKS, :] = jnp.full((CHUNKS, LANES), rank, F32)
        low = INSIDE.start + i * CHUNKS
        info_ref[low : low + CHUNKS, :] = (start - chunk_row).astype(F32)


def pitched(row, span):
    return row + lax.div(row, span)


def fetch_kernel(rows, lengths_hbm, k_hbm, v_hbm, q_hbm, res_hbm, taps_hbm, k_ref, v_ref, q_next, r_next, taps_ref, info_ref, lengths_ref, sems):
    columns = pl.ds(0, q_next.shape[1])
    pairs = (
        (lengths_hbm, lengths_ref),
        (k_hbm, k_ref),
        (v_hbm, v_ref),
        (q_hbm.at[:, columns], q_next),
        (res_hbm.at[:, columns], r_next),
        (taps_hbm, taps_ref),
    )
    copies = [pltpu.make_async_copy(source, target, sems.at[i]) for i, (source, target) in enumerate(pairs)]
    for copy in copies:
        copy.start()
    copies[0].wait()
    describe(starts_of(lengths_ref), lax.axis_index("ctx") * rows, rows, info_ref)
    for copy in copies[1:]:
        copy.wait()


def end_kernel(rows, poles, info_ref, k_ref, v_ref, taps_ref, rate_ref, gated_a, gated_hbm, end_ref, gated_b, kx, vx, gx, decay_ref, mends, out_sems):
    span = rows // CHUNKS
    phase = lax.broadcasted_iota(jnp.int32, (CHUNKS, LANES), 0)
    groups = k_ref.shape[1] // GROUP
    last = jnp.int32(0)
    mended = jnp.int32(0)
    for i in range(SEGMENTS):
        low = INSIDE.start + i * CHUNKS
        inside = jnp.max(info_ref[low : low + 1, :]).astype(jnp.int32)
        here_now = (inside >= 0) & (inside < rows)
        last = jnp.where(here_now, inside, last)
        for row, reach, wanted in (
            (inside, 0, here_now),
            (inside + 1, 1, (inside >= -1) & (inside < rows - 1)),
        ):
            mends[0, mended] = jnp.where(wanted, row, 0)
            mends[1, mended] = reach
            mended = mended + wanted.astype(jnp.int32)
    inner = GROUP // LANES

    def store(here):
        return pltpu.make_async_copy(gated_b.at[here], gated_hbm.at[here], out_sems.at[here])

    def one_group(group, first, gated_ref):
        @pl.loop(group * inner, (group + 1) * inner)
        def _(part):
            lanes = lanes_at(part)
            here = part - first * inner
            for i, source, target in ((1, k_ref, kx), (2, v_ref, vx)):
                target[6:8, :] = jnp.zeros((2, LANES), F32)
                target[8:, :] = source[:, lanes].astype(F32)
            decay_ref[...] = jnp.exp(-float(CHUNKS) * rate_ref[:, lanes])
            lines = [[taps_ref[i, j : j + 1, lanes] for j in range(3)] for i in (1, 2)]
            taps = [[spread(line) for line in three] for three in lines]
            for block in range(rows // CHUNKS):
                low = block * CHUNKS
                shorts = []
                for three, source in zip(taps, (kx, vx)):
                    short = three[0] * source[low + 8 : low + 16, :]
                    for back in (1, 2):
                        short = short + three[back] * source[low + 8 - back : low + 16 - back, :]
                    shorts.append(short)
                gated = shorts[0] * shorts[1]
                gx[low : low + CHUNKS, :] = gated
                to = low + low // span
                gated_ref[here, to : to + CHUNKS, :] = gated

            @pl.when(mended > 0)
            def _():
                @pl.loop(0, mended)
                def _(i):
                    row = mends[0, i]
                    reach = mends[1, i].astype(F32)
                    shorts = []
                    for three, source in zip(lines, (kx, vx)):
                        now = three[0] * source[pl.ds(row + 8, 1), :]
                        shorts.append(now + three[1] * source[pl.ds(row + 7, 1), :] * reach)
                    gated = shorts[0] * shorts[1]
                    gx[pl.ds(row, 1), :] = gated
                    gated_ref[here, pl.ds(pitched(row, span), 1), :] = gated

                for block in range(rows // CHUNKS):
                    low = block * CHUNKS
                    gx[low : low + CHUNKS, :] = jnp.where(
                        phase + low >= last, gx[low : low + CHUNKS, :], 0.0
                    )

            decay = [spread(decay_ref[m : m + 1, :]) for m in range(poles)]
            sums = [gx[:CHUNKS, :] for _ in range(poles)]
            for block in range(1, rows // CHUNKS):
                gated = gx[block * CHUNKS : (block + 1) * CHUNKS, :]
                sums = [decay[m] * sums[m] + gated for m in range(poles)]
            after = (phase - (CHUNKS - 1)).astype(F32)
            for m in range(poles):
                weight = jnp.exp(after * spread(rate_ref[m : m + 1, lanes]))
                end_ref[part, m : m + 1, :] = jnp.sum(weight * sums[m], axis=0, keepdims=True)
            if first:
                store(here).start()

    middle = gated_a.shape[0] // inner
    pl.loop(middle, groups)(lambda group: one_group(group, middle, gated_b))
    pl.loop(0, middle)(lambda group: one_group(group, 0, gated_a))
    for here in range(gated_b.shape[0]):
        store(here).wait()


def edge_kernel(rows, poles, info_ref, k_ref, v_ref, rim_ref, taps_ref, rate_ref, partial_ref, end_hbm, edge_ref, rim_next, taps_next, end_ref, sems):
    rim_next[...] = rim_ref[0]
    taps_next[...] = taps_ref[0]
    clear = [jnp.ones((1, LANES), F32) for _ in range(4)]
    for i in range(SEGMENTS):
        low = INSIDE.start + i * CHUNKS
        inside = info_ref[low : low + 1, :]
        for j, (first, last) in enumerate(((0, 0), (-1, -1), (1, 1), (1, rows - 1))):
            clear[j] = jnp.where((inside >= float(first)) & (inside <= float(last)), 0.0, clear[j])
    at_zero, at_before, at_one, after = clear
    inner = GROUP // LANES

    def send(group):
        here = pl.ds(group * inner, inner)
        return pltpu.make_async_copy(end_ref.at[here], end_hbm.at[here], sems.at[group])

    @pl.loop(0, sems.shape[0])
    def _(group):
        @pl.loop(group * inner, (group + 1) * inner)
        def _(part):
            lanes = lanes_at(part)
            own = [[], []]
            full = [[], []]
            for i, source in ((1, k_ref), (2, v_ref)):
                taps = [taps_ref[i, j : j + 1, lanes] for j in range(3)]
                top = source[:16, lanes].astype(F32)
                rim = rim_ref[i, :, lanes].astype(F32)
                zero, one, back, far = top[0:1], top[1:2], rim[1:2], rim[0:1]
                own[0].append(taps[0] * zero)
                own[1].append(taps[0] * one + at_one * (taps[1] * zero))
                full[0].append(own[0][-1] + at_zero * (taps[1] * back + at_before * (taps[2] * far)))
                full[1].append(own[1][-1] + (at_one * at_zero) * (taps[2] * back))
            made = [full[row][0] * full[row][1] for row in range(2)]
            change = [after * (made[row] - own[row][0] * own[row][1]) for row in range(2)]
            for row in range(2):
                edge_ref[part, row : row + 1, :] = made[row]
            rate = rate_ref[:, lanes]
            end_ref[part] = (
                partial_ref[part]
                + jnp.exp(-float(rows - 1) * rate) * change[0]
                + jnp.exp(-float(rows - 2) * rate) * change[1]
            )

        send(group).start()

    for group in range(sems.shape[0]):
        send(group).wait()


def rank_factors(info_ref, rows, poles, rate_ref, out_ref):
    ranks, held = out_ref.shape[:2]
    shares = poles // held
    mine = lax.axis_index("ctx")
    lanes = lanes_at(lax.div(mine, shares))
    rate = rate_ref[:held, lanes]
    for share in range(1, shares):
        theirs = rate_ref[share * held : (share + 1) * held, lanes]
        rate = jnp.where(lax.rem(mine, shares) == share, theirs, rate)
    whole = jnp.exp(-float(rows) * rate)
    begun = [info_ref[BEGUN.start + i * CHUNKS : BEGUN.start + i * CHUNKS + held, :] for i in range(1, SEGMENTS)]
    for rank in range(ranks):
        kept = whole
        for begin in begun:
            kept = jnp.where(begin == float(rank), 0.0, kept)
        out_ref[rank] = kept


def scan_kernel(factor_ref, pieces_ref, out_hbm, out_ref, sems):
    running = jnp.zeros(pieces_ref.shape[1:], F32)
    ranks = pieces_ref.shape[0]
    block = ranks // sems.shape[0]
    copies = []
    for rank in range(ranks):
        out_ref[rank] = running
        running = factor_ref[rank] * running + pieces_ref[rank]
        if rank % block == block - 1:
            here = pl.ds(rank - block + 1, block)
            copies.append(pltpu.make_async_copy(out_ref.at[here], out_hbm.at[here], sems.at[rank // block]))
            copies[-1].start()
    for copy in copies:
        copy.wait()


def near_kernel(rows, poles, first, early, info_ref, rim_ref, taps_ref, rate_ref, gain_ref, skip_ref, edge_ref, gated_in, q_in, r_in, q_hbm, res_hbm, gated_hbm, *others):
    if early:
        outs, (factor_ref, gated_next, q_next, r_next, *others) = others[:3], others[3:]
        near_ref, query_ref, local_ref, q_ref, r_ref, qx, rx, decay_ref, own_sems, far_sems, next_sems = others
        gated_ref = gated_in
        count = near_ref.shape[0]
    else:
        heads, tails, others = others[:3], others[3:6], others[6:]
        gated_ref, near_ref, query_ref, local_ref, q_ref, r_ref, qx, rx, decay_ref, own_sems, far_sems = others
        count = near_ref.shape[0]

    cuts = ((HEAD, NEXT), (NEXT, count))

    def fetch(cut):
        low, high = cuts[cut]
        from_columns = pl.ds((first + low) * LANES, (high - low) * LANES)
        columns = pl.ds(low * LANES, (high - low) * LANES)
        pairs = [(source.at[:, from_columns], target.at[:, columns]) for source, target in ((q_hbm, q_ref), (res_hbm, r_ref))]
        if not early:
            blocks = pl.ds(low, high - low)
            pairs.append((gated_hbm.at[blocks], gated_ref.at[blocks]))
        return [
            pltpu.make_async_copy(source, target, own_sems.at[i, cut])
            for i, (source, target) in enumerate(pairs)
        ]

    for cut in range(len(cuts)):
        for copy in fetch(cut):
            copy.start()
    for i, (source, target) in enumerate(((q_in, q_ref), (r_in, r_ref))):
        target[:, : HEAD * LANES] = source[...]
    if early:
        columns = pl.ds((first + count) * LANES, HEAD * LANES)
        pairs = (
            (gated_hbm.at[pl.ds(0, HEAD)], gated_next),
            (q_hbm.at[:, columns], q_next),
            (res_hbm.at[:, columns], r_next),
        )
        ahead_of_time = [
            pltpu.make_async_copy(source, target, next_sems.at[i]) for i, (source, target) in enumerate(pairs)
        ]
        for copy in ahead_of_time:
            copy.start()
        rank_factors(info_ref, rows, poles, rate_ref, factor_ref)
    else:
        gated_ref[:HEAD] = gated_in[...]
    span = rows // CHUNKS
    chunk = lax.broadcasted_iota(jnp.int32, (CHUNKS, LANES), 0)
    flags = [
        jnp.max(info_ref[FLAGS.start + block : FLAGS.start + block + 1, :]) > 0.0
        for block in range(span // STEPS)
    ]

    made = (near_ref, query_ref, local_ref)

    def store(here, targets, low):
        return [
            pltpu.make_async_copy(source.at[here], target.at[here - low], far_sems.at[i, here])
            for i, (source, target) in enumerate(zip(made, targets))
        ]

    @pl.loop(0, count)
    def _(here):
        own = lanes_at(here)
        lanes = lanes_at(here + first)
        far = info_ref[FAR, :]
        joined = info_ref[JOINED, :]

        for cut, (low, _) in enumerate(cuts):

            @pl.when(here == low)
            def _():
                for copy in fetch(cut):
                    copy.wait()

        qx[5:7, :] = rim_ref[:, lanes].astype(F32)
        lay_out(q_ref, own, qx, span, 8)
        lay_out(r_ref, own, rx, span, 0)
        decay_ref[...] = jnp.exp(-rate_ref[:, lanes])
        taps = [spread(taps_ref[j : j + 1, lanes]) for j in range(3)]
        skip = spread(skip_ref[:, lanes])
        decay = [spread(decay_ref[m : m + 1, :]) for m in range(poles)]
        gain = [spread(gain_ref[m : m + 1, lanes]) for m in range(poles)]
        carry = [
            qx[pl.ds(6, CHUNKS, stride=span + 1), :],
            qx[pl.ds(5, CHUNKS, stride=span + 1), :] * far,
        ] + [jnp.zeros((CHUNKS, LANES), F32)] * poles

        def run(block, masked, carry):
            carry = list(carry)
            for step in range(STEPS):
                place = block * STEPS + step
                if masked:
                    keep = jnp.ones((CHUNKS, LANES), F32)
                    for i in range(SEGMENTS):
                        low = INSIDE.start + i * CHUNKS
                        keep = jnp.where(info_ref[low : low + CHUNKS, :] == float(place), 0.0, keep)
                    carry = [held * keep for held in carry]
                query = qx[pl.ds(8 + place, CHUNKS, stride=span + 1), :]
                query_short = taps[0] * query + taps[1] * carry[0] + taps[2] * carry[1]
                gated = gated_ref[here, pl.ds(place, CHUNKS, stride=span + 1), :]
                if place < 2:
                    edge = spread(edge_ref[here + first, place : place + 1, :])
                    gated = jnp.where(chunk == 0, edge, gated)
                states = [decay[m] * carry[2 + m] + gated for m in range(poles)]
                total = skip * gated
                for m in range(poles):
                    total = total + gain[m] * states[m]
                query_ref[here, chunk_of(place), :] = query_short
                near_ref[here, chunk_of(place), :] = (
                    rx[pl.ds(place, CHUNKS, stride=span + 1), :] + query_short * total
                )
                carry = [query, carry[0]] + states
            return tuple(carry)

        carry = walk(span, flags, run, tuple(carry))
        for m in range(poles):
            reach = jnp.exp(-float(span) * spread(rate_ref[m : m + 1, lanes])) * joined
            state = carry[2 + m]
            for hop in (1, 2, 4):
                state = state + reach * pltpu.roll(state, hop, 0)
                if hop < 4:
                    reach = reach * pltpu.roll(reach, hop, 0)
            local_ref[here, m * CHUNKS : (m + 1) * CHUNKS, :] = jnp.where(
                chunk > 0, pltpu.roll(state, 1, 0), 0.0
            )
        if early:
            for copy in store(here, outs, 0):
                copy.start()
        else:

            @pl.when(here < READY)
            def _():
                for source, target in zip(made, heads):
                    target[here] = source[here]

            @pl.when(here >= READY)
            def _():
                for copy in store(here, tails, READY):
                    copy.start()

    if early:
        for copy in ahead_of_time:
            copy.wait()
    for here in range(0 if early else READY, count):
        for copy in store(here, outs, 0) if early else store(here, tails, READY):
            copy.wait()


def stream_kernel(rows, poles, info_ref, rate_ref, gain_ref, incoming_ref, near_hbm, query_hbm, local_hbm, near_head, query_head, local_head, near_rest, query_rest, local_rest, out_hbm, stream_ref, power_ref, near_a, query_a, local_a, near_b, query_b, local_b, sx, px, decay_ref, sems, far_sems, rest_sems):
    span = rows // CHUNKS
    chunk = lax.broadcasted_iota(jnp.int32, (CHUNKS, LANES), 0)
    px[...] = jnp.zeros_like(px)
    inner = GROUP // LANES
    early = near_a.shape[0]

    def fetch(group):
        here = pl.ds(group * inner, inner)
        pairs = ((near_hbm, near_a), (query_hbm, query_a), (local_hbm, local_a))
        return [
            pltpu.make_async_copy(source.at[here], target.at[here], far_sems.at[i, group])
            for i, (source, target) in enumerate(pairs)
        ]

    pairs = ((near_rest, near_b), (query_rest, query_b), (local_rest, local_b))
    rest = [pltpu.make_async_copy(source, target, rest_sems.at[i]) for i, (source, target) in enumerate(pairs)]
    for group in range(early // inner):
        for copy in fetch(group):
            copy.start()
    for copy in rest:
        copy.start()
    before = (chunk * span).astype(F32)

    def copy_out(group):
        lanes = pl.ds(pl.multiple_of(group * GROUP, GROUP), GROUP)
        return pltpu.make_async_copy(stream_ref.at[:, lanes], out_hbm.at[:, lanes], sems.at[group])

    def one_part(part, near_ref, query_ref, local_ref, place_of):
        lanes = lanes_at(part)
        decay_ref[...] = jnp.exp(-rate_ref[:, lanes])
        decay = [spread(decay_ref[m : m + 1, :]) for m in range(poles)]
        reached = info_ref[REACHED, :]
        ahead = info_ref[AHEAD, :]
        carry = []
        for m in range(poles):
            entering = reached * jnp.exp(-before * spread(rate_ref[m : m + 1, lanes]))
            entering = entering * spread(incoming_ref[part, m : m + 1, :])
            entering = entering + local_ref[place_of, m * CHUNKS : (m + 1) * CHUNKS, :]
            carry.append(spread(gain_ref[m : m + 1, lanes]) * entering)
        for place in range(span):
            carry = [decay[m] * carry[m] for m in range(poles)]
            terms = list(carry)
            while len(terms) > 1:
                terms = [
                    terms[i] + terms[i + 1] if i + 1 < len(terms) else terms[i]
                    for i in range(0, len(terms), 2)
                ]
            carried = jnp.where(ahead > float(place), terms[0], 0.0)
            here = chunk_of(place)
            sx[pl.ds(place, CHUNKS, stride=span + 1), :] = (
                near_ref[place_of, here, :] + query_ref[place_of, here, :] * carried
            )
        for piece in range(CHUNKS):
            low = piece * (span + 1)
            stream = sx[low : low + span, :]
            native = slice(piece * span, (piece + 1) * span)
            stream_ref[native, lanes] = stream
            px[native, :] += stream * stream

    groups = stream_ref.shape[1] // GROUP
    sides = (
        (early, near_head, query_head, local_head),
        (0, near_a, query_a, local_a),
        (early + READY, near_b, query_b, local_b),
    )
    for first, near_ref, query_ref, local_ref in sides:

        @pl.loop(0, near_ref.shape[0] // inner)
        def _(group):
            if near_ref is near_a:
                for copy in fetch(group):
                    copy.wait()
            if near_ref is near_b:
                for copy in rest:
                    copy.wait()

            @pl.loop(group * inner, (group + 1) * inner)
            def _(part):
                one_part(part + first, near_ref, query_ref, local_ref, part)

            if near_ref is not near_b:
                copy_out(group + first // inner).start()

    for piece in range(rows // LANES):
        turned = px[piece * LANES : (piece + 1) * LANES, :].T
        power_ref[piece : piece + 1, :] = jnp.sum(turned, axis=0, keepdims=True)
    for group in range((early + READY) // inner):
        copy_out(group).wait()


def norm_kernel(width, left, power_ref, gain_ref, stream_ref, stream_in, out_hbm, stream_out, scale_ref, buffer, sems, left_sem):
    columns = pl.ds(left, stream_ref.shape[1] - left)
    rest = pltpu.make_async_copy(stream_ref.at[:, columns], stream_out.at[:, columns], left_sem.at[0])
    rest.start()
    scale = lax.rsqrt(jnp.sum(power_ref[...], axis=0) / width + 1e-06)
    for piece in range(scale.shape[0]):
        wide = jnp.broadcast_to(scale[piece : piece + 1, :], (LANES, LANES))
        scale_ref[piece * LANES : (piece + 1) * LANES, :] = wide.T
    rows = stream_ref.shape[0]
    count = sems.shape[0]
    tall = rows // count

    def copy_out(group):
        here = pl.ds(pl.multiple_of(group * tall, tall), tall)
        return pltpu.make_async_copy(buffer.at[here, :], out_hbm.at[here, :], sems.at[group])

    @pl.loop(0, count)
    def _(group):
        here = pl.ds(pl.multiple_of(group * tall, tall), tall)
        factor = scale_ref[here, :]
        for part in range(stream_ref.shape[1] // LANES):
            lanes = slice(part * LANES, (part + 1) * LANES)
            buffer[here, lanes] = stream_ref[here, lanes] * factor * gain_ref[:, lanes]
        copy_out(group).start()

    for group in range(count):
        copy_out(group).wait()
    rest.wait()


def shifted(block, axis, distance):
    count = lax.axis_size(axis)
    return lax.ppermute(block, axis, [(i, (i + distance) % count) for i in range(count)])


def on_device(query_proj, key_proj, value_proj, short_filter, decay_rate, residue, skip_gain, norm_gain, residual, lengths):
    rows, width = query_proj.shape
    poles = decay_rate.shape[0]
    ranks = lax.axis_size("ctx")
    parts = width // LANES
    groups = width // GROUP
    near_by = pl.BlockSpec(memory_space=pltpu.VMEM)
    outside = pl.BlockSpec(memory_space=pltpu.HBM)
    limit = pltpu.CompilerParams(vmem_limit_bytes=12 * 1024 * 1024)
    shape = lambda *dims: jax.ShapeDtypeStruct(dims, F32)
    kept_near = lambda *dims: pltpu.VMEM(dims, F32)
    far_off = lambda array: pltpu.with_memory_space_constraint(array, pltpu.HBM)
    close_by = lambda array: pltpu.with_memory_space_constraint(array, pltpu.VMEM)
    query_proj, key_proj, value_proj, residual, short_filter, lengths = map(
        far_off, (query_proj, key_proj, value_proj, residual, short_filter, lengths)
    )

    rims = pl.pallas_call(
        rim_kernel,
        in_specs=[outside] * 3,
        out_specs=near_by,
        out_shape=pltpu.VMEM((3, 2, width), BF16),
        scratch_shapes=[pltpu.VMEM((3, 16, width), BF16), pltpu.SemaphoreType.DMA((3,))],
        name="rims",
    )(query_proj, key_proj, value_proj)
    rims = shifted(rims, "ctx", 1)
    pole_gain = residue * jnp.sqrt(-jnp.expm1(-2.0 * decay_rate))
    skip = skip_gain.reshape(1, width)

    early = FIRST_SHARE * (GROUP // LANES)
    late = parts - early
    pitch = rows + CHUNKS
    held = parts * poles // ranks
    k_here, v_here, q_a, r_a, taps_here, info = pl.pallas_call(
        functools.partial(fetch_kernel, rows),
        in_specs=[outside] * 6,
        out_specs=[near_by] * 6,
        out_shape=[
            pltpu.VMEM((rows, width), BF16),
            pltpu.VMEM((rows, width), BF16),
            pltpu.VMEM((rows, HEAD * LANES), BF16),
            pltpu.VMEM((rows, HEAD * LANES), BF16),
            kept_near(3, 3, width),
            kept_near(SECTIONS, LANES),
        ],
        scratch_shapes=[pltpu.SMEM(lengths.shape, jnp.int32), pltpu.SemaphoreType.DMA((6,))],
        compiler_params=limit,
        cost_estimate=pl.CostEstimate(flops=1000000, bytes_accessed=5000000, transcendentals=0),
        name="fetch",
    )(lengths, key_proj, value_proj, query_proj, residual, short_filter)
    info, k_here, v_here, taps_here = map(close_by, (info, k_here, v_here, taps_here))
    gated_a, gated_b, partial = pl.pallas_call(
        functools.partial(end_kernel, rows, poles),
        in_specs=[near_by] * 5,
        out_specs=[near_by, outside, near_by],
        out_shape=[
            kept_near(early, pitch, LANES),
            pltpu.HBM((late, pitch, LANES), F32),
            kept_near(parts, poles, LANES),
        ],
        scratch_shapes=[
            pltpu.VMEM((late, pitch, LANES), F32),
            pltpu.VMEM((rows + 8, LANES), F32),
            pltpu.VMEM((rows + 8, LANES), F32),
            pltpu.VMEM((rows, LANES), F32),
            pltpu.VMEM((poles, LANES), F32),
            pltpu.SMEM((2, 8), jnp.int32),
            pltpu.SemaphoreType.DMA((late,)),
        ],
        compiler_params=limit,
        cost_estimate=pl.CostEstimate(flops=4000000, bytes_accessed=8000000, transcendentals=0),
        name="end_state",
    )(info, k_here, v_here, taps_here, decay_rate)
    end, edges, query_rim, query_taps = pl.pallas_call(
        functools.partial(edge_kernel, rows, poles),
        in_specs=[near_by] * 7,
        out_specs=[outside, near_by, near_by, near_by],
        out_shape=[
            pltpu.HBM((parts, poles, LANES), F32),
            kept_near(parts, CHUNKS, LANES),
            pltpu.VMEM((2, width), BF16),
            kept_near(3, width),
        ],
        scratch_shapes=[pltpu.VMEM((parts, poles, LANES), F32), pltpu.SemaphoreType.DMA((groups,))],
        compiler_params=limit,
        name="edges",
    )(info, k_here, v_here, rims, taps_here, decay_rate, close_by(partial))
    edges = close_by(edges)
    query_rim, query_taps = map(close_by, (query_rim, query_taps))

    pieces = lax.all_to_all(end.reshape(ranks, held, LANES), "ctx", 0, 0, tiled=True)

    def near_side(first, count, gated, q_part, r_part, early):
        block = (count, rows, LANES)
        states = (count, poles * CHUNKS, LANES)
        given = [info, query_rim, query_taps, decay_rate, pole_gain, skip, edges, *map(close_by, (gated, q_part, r_part))]
        fetched = [query_proj, residual, far_off(gated_b)]
        scratch = [
            pltpu.VMEM((rows, count * LANES), BF16),
            pltpu.VMEM((rows, count * LANES), BF16),
            pltpu.VMEM((rows + 16, LANES), F32),
            pltpu.VMEM((rows + 16, LANES), F32),
            pltpu.VMEM((poles, LANES), F32),
            pltpu.SemaphoreType.DMA((3, 2)),
            pltpu.SemaphoreType.DMA((3, count)),
        ]
        if early:
            out_specs = [outside] * 3 + [near_by] * 4
            out_shape = [pltpu.HBM(dims, F32) for dims in (block, block, states)] + [
                kept_near(ranks, held, LANES),
                kept_near(HEAD, pitch, LANES),
                pltpu.VMEM((rows, HEAD * LANES), BF16),
                pltpu.VMEM((rows, HEAD * LANES), BF16),
            ]
            scratch = [pltpu.VMEM(dims, F32) for dims in (block, block, states)] + scratch
            scratch += [pltpu.SemaphoreType.DMA((3,))]
        else:
            out_specs = [near_by] * 3 + [outside] * 3
            out_shape = [kept_near(READY, *dims[1:]) for dims in (block, block, states)]
            out_shape += [pltpu.HBM((count - READY, *dims[1:]), F32) for dims in (block, block, states)]
            scratch = [pltpu.VMEM(dims, F32) for dims in ((count, pitch, LANES), block, block, states)] + scratch
        return pl.pallas_call(
            functools.partial(near_kernel, rows, poles, first, early),
            in_specs=[near_by] * len(given) + [outside] * len(fetched),
            out_specs=out_specs,
            out_shape=out_shape,
            scratch_shapes=scratch,
            compiler_params=limit,
            cost_estimate=pl.CostEstimate(flops=4000000, bytes_accessed=8000000, transcendentals=0),
            name="near",
        )(*given, *fetched)

    near_a, query_a, local_a, factors, gated_head, q_b, r_b = near_side(0, early, gated_a, q_a, r_a, True)
    near_b = near_side(early, late, gated_head, q_b, r_b, False)
    scanned = pl.pallas_call(
        scan_kernel,
        in_specs=[near_by, near_by],
        out_specs=outside,
        out_shape=pltpu.HBM((ranks, held, LANES), F32),
        scratch_shapes=[pltpu.VMEM((ranks, held, LANES), F32), pltpu.SemaphoreType.DMA((2,))],
        compiler_params=limit,
        name="rank_scan",
    )(close_by(factors), pieces)
    incoming = lax.all_to_all(scanned, "ctx", 0, 0, tiled=True).reshape(parts, poles, LANES)

    stream, kept, power = pl.pallas_call(
        functools.partial(stream_kernel, rows, poles),
        in_specs=[near_by] * 4 + [outside] * 3 + [near_by] * 3 + [outside] * 3,
        out_specs=[outside, near_by, near_by],
        out_shape=[pltpu.HBM((rows, width), F32), kept_near(rows, width), kept_near(rows // LANES, LANES)],
        scratch_shapes=[
            pltpu.VMEM((early, rows, LANES), F32),
            pltpu.VMEM((early, rows, LANES), F32),
            pltpu.VMEM((early, poles * CHUNKS, LANES), F32),
            pltpu.VMEM((late - READY, rows, LANES), F32),
            pltpu.VMEM((late - READY, rows, LANES), F32),
            pltpu.VMEM((late - READY, poles * CHUNKS, LANES), F32),
            pltpu.VMEM((rows + 8, LANES), F32),
            pltpu.VMEM((rows, LANES), F32),
            pltpu.VMEM((poles, LANES), F32),
            pltpu.SemaphoreType.DMA((groups,)),
            pltpu.SemaphoreType.DMA((3, early // (GROUP // LANES))),
            pltpu.SemaphoreType.DMA((3,)),
        ],
        compiler_params=limit,
        name="stream",
    )(
        info,
        decay_rate,
        pole_gain,
        incoming,
        *map(far_off, (near_a, query_a, local_a)),
        *map(close_by, near_b[:3]),
        *map(far_off, near_b[3:]),
    )
    shares = lax.axis_size("ch")
    near_first = sorted(range(1, shares), key=lambda hop: min(hop, shares - hop))
    powers = jnp.stack([power] + [shifted(power, "ch", hop) for hop in near_first])
    normed, stream = pl.pallas_call(
        functools.partial(norm_kernel, float(width * shares), (early + READY) * LANES),
        in_specs=[near_by, near_by, near_by, outside],
        out_specs=[outside, outside],
        out_shape=[pltpu.HBM((rows, width), F32)] * 2,
        input_output_aliases={3: 1},
        scratch_shapes=[
            pltpu.VMEM((rows, LANES), F32),
            pltpu.VMEM((rows, width), F32),
            pltpu.SemaphoreType.DMA((8,)),
            pltpu.SemaphoreType.DMA((1,)),
        ],
        compiler_params=limit,
        name="norm",
    )(powers, norm_gain.reshape(1, width), close_by(kept), far_off(stream))
    return (stream, normed)


def solution(mesh):
    placed = (
        P("ctx", "ch"),
        P("ctx", "ch"),
        P("ctx", "ch"),
        P(None, None, "ch"),
        P(None, "ch"),
        P(None, "ch"),
        P("ch"),
        P("ch"),
        P("ctx", "ch"),
        P(),
    )
    return jax.shard_map(
        on_device,
        mesh=mesh,
        in_specs=placed,
        out_specs=(P("ctx", "ch"), P("ctx", "ch")),
        check_vma=False,
    )
```

```python
import functools

import jax
import jax.numpy as jnp
from jax import lax
from jax.experimental import pallas as pl
from jax.experimental.pallas import tpu as pltpu
from jax.sharding import PartitionSpec as P

LANES = 128
CHUNKS = 8
GROUP = 256
FIRST_SHARE = 4
HEAD = 2
NEXT = 4
READY = 6
STEPS = 16
F32 = jnp.float32
BF16 = jnp.bfloat16


def starts_of(lengths_ref):
    first = lengths_ref[0]
    second = first + lengths_ref[1]
    third = second + lengths_ref[2]
    return (jnp.int32(0), first, second, third)


def spread(row):
    return jnp.broadcast_to(row, (CHUNKS, LANES))


def no_start(starts, where):
    kept = jnp.ones(where.shape, jnp.bool_)
    for start in starts:
        kept = kept & (where != start)
    return kept.astype(F32)


def any_in(starts, low, high):
    found = jnp.bool_(False)
    for start in starts:
        found = found | ((start >= low) & (start < high))
    return found


def block_has_start(starts, base, rows, block):
    found = jnp.bool_(False)
    for start in starts:
        inside = start - base
        place = lax.rem(jnp.maximum(inside, 0), rows // CHUNKS)
        found = found | (
            (inside >= 0) & (inside < rows) & (place >= block * STEPS) & (place < (block + 1) * STEPS)
        )
    return found


def lanes_at(part):
    return pl.ds(pl.multiple_of(part * LANES, LANES), LANES)


def chunk_of(place):
    return pl.ds(pl.multiple_of(place * CHUNKS, CHUNKS), CHUNKS)


def lay_out(source, lanes, target, span, offset):
    for piece in range(CHUNKS):
        low = offset + piece * (span + 1)
        target[low : low + span, :] = source[piece * span : (piece + 1) * span, lanes].astype(F32)


def rim_kernel(q_hbm, k_hbm, v_hbm, out_ref, buffer, sems):
    tail = buffer.shape[1]
    copies = [
        pltpu.make_async_copy(source.at[pl.ds(source.shape[0] - tail, tail), :], buffer.at[i], sems.at[i])
        for i, source in enumerate((q_hbm, k_hbm, v_hbm))
    ]
    for copy in copies:
        copy.start()
    for i, copy in enumerate(copies):
        copy.wait()
        out_ref[i] = buffer[i, tail - 2 :, :]


def walk(span, flags, run, carry):
    for block in range(span // STEPS):
        carry = lax.cond(
            flags[block], functools.partial(run, block, True), functools.partial(run, block, False), carry
        )
    return carry


SEGMENTS = 4
FAR, JOINED, REACHED, AHEAD, FLAGS, BEGUN, INSIDE = (slice(i * CHUNKS, (i + 1) * CHUNKS) for i in (0, 1, 2, 3, 4, 5, 5 + SEGMENTS))
SECTIONS = (5 + 2 * SEGMENTS) * CHUNKS


def describe(starts, base, rows, info_ref):
    span = rows // CHUNKS
    chunk = lax.broadcasted_iota(jnp.int32, (CHUNKS, LANES), 0)
    chunk_row = base + chunk * span
    alive = jnp.ones((CHUNKS, LANES), jnp.bool_)
    reached = jnp.ones((CHUNKS, LANES), jnp.bool_)
    ahead = jnp.full((CHUNKS, LANES), span, jnp.int32)
    for start in starts:
        inside = start - chunk_row
        alive = alive & ((inside < 0) | (inside >= span))
        reached = reached & ((start < base) | (inside >= 0))
        ahead = jnp.where((inside >= 0) & (inside < ahead), inside, ahead)
    info_ref[FAR, :] = no_start(starts, chunk_row - 1)
    info_ref[JOINED, :] = (alive & (chunk > 0)).astype(F32)
    info_ref[REACHED, :] = reached.astype(F32)
    info_ref[AHEAD, :] = ahead.astype(F32)
    for block in range(span // STEPS):
        flag = jnp.where(block_has_start(starts, base, rows, block), 1.0, 0.0)
        info_ref[FLAGS.start + block : FLAGS.start + block + 1, :] = jnp.full((1, LANES), flag, F32)
    for i, start in enumerate(starts):
        rank = lax.div(start, rows).astype(F32)
        low = BEGUN.start + i * CHUNKS
        info_ref[low : low + CHUNKS, :] = jnp.full((CHUNKS, LANES), rank, F32)
        low = INSIDE.start + i * CHUNKS
        info_ref[low : low + CHUNKS, :] = (start - chunk_row).astype(F32)


def pitched(row, span):
    return row + lax.div(row, span)


def fetch_kernel(rows, lengths_hbm, k_hbm, v_hbm, q_hbm, res_hbm, taps_hbm, k_ref, v_ref, q_next, r_next, taps_ref, info_ref, lengths_ref, sems):
    columns = pl.ds(0, q_next.shape[1])
    pairs = (
        (lengths_hbm, lengths_ref),
        (k_hbm, k_ref),
        (v_hbm, v_ref),
        (q_hbm.at[:, columns], q_next),
        (res_hbm.at[:, columns], r_next),
        (taps_hbm, taps_ref),
    )
    copies = [pltpu.make_async_copy(source, target, sems.at[i]) for i, (source, target) in enumerate(pairs)]
    for copy in copies:
        copy.start()
    copies[0].wait()
    describe(starts_of(lengths_ref), lax.axis_index("ctx") * rows, rows, info_ref)
    for copy in copies[1:]:
        copy.wait()


def end_kernel(rows, poles, info_ref, k_ref, v_ref, taps_ref, rate_ref, gated_a, gated_hbm, end_ref, gated_b, kx, vx, gx, decay_ref, mends, out_sems):
    span = rows // CHUNKS
    phase = lax.broadcasted_iota(jnp.int32, (CHUNKS, LANES), 0)
    groups = k_ref.shape[1] // GROUP
    last = jnp.int32(0)
    mended = jnp.int32(0)
    for i in range(SEGMENTS):
        low = INSIDE.start + i * CHUNKS
        inside = jnp.max(info_ref[low : low + 1, :]).astype(jnp.int32)
        here_now = (inside >= 0) & (inside < rows)
        last = jnp.where(here_now, inside, last)
        for row, reach, wanted in (
            (inside, 0, here_now),
            (inside + 1, 1, (inside >= -1) & (inside < rows - 1)),
        ):
            mends[0, mended] = jnp.where(wanted, row, 0)
            mends[1, mended] = reach
            mended = mended + wanted.astype(jnp.int32)
    inner = GROUP // LANES

    def store(here):
        return pltpu.make_async_copy(gated_b.at[here], gated_hbm.at[here], out_sems.at[here])

    def one_group(group, first, gated_ref):
        @pl.loop(group * inner, (group + 1) * inner)
        def _(part):
            lanes = lanes_at(part)
            here = part - first * inner
            for i, source, target in ((1, k_ref, kx), (2, v_ref, vx)):
                target[6:8, :] = jnp.zeros((2, LANES), F32)
                target[8:, :] = source[:, lanes].astype(F32)
            decay_ref[...] = jnp.exp(-float(CHUNKS) * rate_ref[:, lanes])
            lines = [[taps_ref[i, j : j + 1, lanes] for j in range(3)] for i in (1, 2)]
            taps = [[spread(line) for line in three] for three in lines]
            for block in range(rows // CHUNKS):
                low = block * CHUNKS
                shorts = []
                for three, source in zip(taps, (kx, vx)):
                    short = three[0] * source[low + 8 : low + 16, :]
                    for back in (1, 2):
                        short = short + three[back] * source[low + 8 - back : low + 16 - back, :]
                    shorts.append(short)
                gated = shorts[0] * shorts[1]
                gx[low : low + CHUNKS, :] = gated
                to = low + low // span
                gated_ref[here, to : to + CHUNKS, :] = gated

            @pl.when(mended > 0)
            def _():
                @pl.loop(0, mended)
                def _(i):
                    row = mends[0, i]
                    reach = mends[1, i].astype(F32)
                    shorts = []
                    for three, source in zip(lines, (kx, vx)):
                        now = three[0] * source[pl.ds(row + 8, 1), :]
                        shorts.append(now + three[1] * source[pl.ds(row + 7, 1), :] * reach)
                    gated = shorts[0] * shorts[1]
                    gx[pl.ds(row, 1), :] = gated
                    gated_ref[here, pl.ds(pitched(row, span), 1), :] = gated

                for block in range(rows // CHUNKS):
                    low = block * CHUNKS
                    gx[low : low + CHUNKS, :] = jnp.where(
                        phase + low >= last, gx[low : low + CHUNKS, :], 0.0
                    )

            decay = [spread(decay_ref[m : m + 1, :]) for m in range(poles)]
            sums = [gx[:CHUNKS, :] for _ in range(poles)]
            for block in range(1, rows // CHUNKS):
                gated = gx[block * CHUNKS : (block + 1) * CHUNKS, :]
                sums = [decay[m] * sums[m] + gated for m in range(poles)]
            after = (phase - (CHUNKS - 1)).astype(F32)
            for m in range(poles):
                weight = jnp.exp(after * spread(rate_ref[m : m + 1, lanes]))
                end_ref[part, m : m + 1, :] = jnp.sum(weight * sums[m], axis=0, keepdims=True)
            if first:
                store(here).start()

    middle = gated_a.shape[0] // inner
    pl.loop(middle, groups)(lambda group: one_group(group, middle, gated_b))
    pl.loop(0, middle)(lambda group: one_group(group, 0, gated_a))
    for here in range(gated_b.shape[0]):
        store(here).wait()


def edge_kernel(rows, poles, info_ref, k_ref, v_ref, rim_ref, taps_ref, rate_ref, partial_ref, end_hbm, edge_ref, rim_next, taps_next, end_ref, sems):
    rim_next[...] = rim_ref[0]
    taps_next[...] = taps_ref[0]
    clear = [jnp.ones((1, LANES), F32) for _ in range(4)]
    for i in range(SEGMENTS):
        low = INSIDE.start + i * CHUNKS
        inside = info_ref[low : low + 1, :]
        for j, (first, last) in enumerate(((0, 0), (-1, -1), (1, 1), (1, rows - 1))):
            clear[j] = jnp.where((inside >= float(first)) & (inside <= float(last)), 0.0, clear[j])
    at_zero, at_before, at_one, after = clear
    inner = GROUP // LANES

    def send(group):
        here = pl.ds(group * inner, inner)
        return pltpu.make_async_copy(end_ref.at[here], end_hbm.at[here], sems.at[group])

    for group in range(sems.shape[0]):
        for part in range(group * inner, (group + 1) * inner):
            lanes = slice(part * LANES, (part + 1) * LANES)
            own = [[], []]
            full = [[], []]
            for i, source in ((1, k_ref), (2, v_ref)):
                taps = [taps_ref[i, j : j + 1, lanes] for j in range(3)]
                top = source[:16, lanes].astype(F32)
                rim = rim_ref[i, :, lanes].astype(F32)
                zero, one, back, far = top[0:1], top[1:2], rim[1:2], rim[0:1]
                own[0].append(taps[0] * zero)
                own[1].append(taps[0] * one + at_one * (taps[1] * zero))
                full[0].append(own[0][-1] + at_zero * (taps[1] * back + at_before * (taps[2] * far)))
                full[1].append(own[1][-1] + (at_one * at_zero) * (taps[2] * back))
            made = [full[row][0] * full[row][1] for row in range(2)]
            change = [after * (made[row] - own[row][0] * own[row][1]) for row in range(2)]
            for row in range(2):
                edge_ref[part, row : row + 1, :] = made[row]
            rate = rate_ref[:, lanes]
            end_ref[part] = (
                partial_ref[part]
                + jnp.exp(-float(rows - 1) * rate) * change[0]
                + jnp.exp(-float(rows - 2) * rate) * change[1]
            )

        send(group).start()

    for group in range(sems.shape[0]):
        send(group).wait()


def rank_factors(info_ref, rows, poles, rate_ref, out_ref):
    ranks, held = out_ref.shape[:2]
    shares = poles // held
    mine = lax.axis_index("ctx")
    lanes = lanes_at(lax.div(mine, shares))
    rate = rate_ref[:held, lanes]
    for share in range(1, shares):
        theirs = rate_ref[share * held : (share + 1) * held, lanes]
        rate = jnp.where(lax.rem(mine, shares) == share, theirs, rate)
    whole = jnp.exp(-float(rows) * rate)
    begun = [info_ref[BEGUN.start + i * CHUNKS : BEGUN.start + i * CHUNKS + held, :] for i in range(1, SEGMENTS)]
    for rank in range(ranks):
        kept = whole
        for begin in begun:
            kept = jnp.where(begin == float(rank), 0.0, kept)
        out_ref[rank] = kept


def scan_kernel(factor_ref, pieces_ref, out_hbm, out_ref, sems):
    running = jnp.zeros(pieces_ref.shape[1:], F32)
    ranks = pieces_ref.shape[0]
    block = ranks // sems.shape[0]
    copies = []
    for rank in range(ranks):
        out_ref[rank] = running
        running = factor_ref[rank] * running + pieces_ref[rank]
        if rank % block == block - 1:
            here = pl.ds(rank - block + 1, block)
            copies.append(pltpu.make_async_copy(out_ref.at[here], out_hbm.at[here], sems.at[rank // block]))
            copies[-1].start()
    for copy in copies:
        copy.wait()


def near_kernel(rows, poles, first, early, info_ref, rim_ref, taps_ref, rate_ref, gain_ref, skip_ref, edge_ref, gated_in, q_in, r_in, q_hbm, res_hbm, gated_hbm, *others):
    if early:
        outs, (factor_ref, gated_next, q_next, r_next, *others) = others[:3], others[3:]
        near_ref, query_ref, local_ref, q_ref, r_ref, qx, rx, decay_ref, own_sems, far_sems, next_sems = others
        gated_ref = gated_in
        count = near_ref.shape[0]
    else:
        heads, tails, others = others[:3], others[3:6], others[6:]
        gated_ref, near_ref, query_ref, local_ref, q_ref, r_ref, qx, rx, decay_ref, own_sems, far_sems = others
        count = near_ref.shape[0]

    cuts = ((HEAD, NEXT), (NEXT, count))

    def fetch(cut):
        low, high = cuts[cut]
        from_columns = pl.ds((first + low) * LANES, (high - low) * LANES)
        columns = pl.ds(low * LANES, (high - low) * LANES)
        pairs = [(source.at[:, from_columns], target.at[:, columns]) for source, target in ((q_hbm, q_ref), (res_hbm, r_ref))]
        if not early:
            blocks = pl.ds(low, high - low)
            pairs.append((gated_hbm.at[blocks], gated_ref.at[blocks]))
        return [
            pltpu.make_async_copy(source, target, own_sems.at[i, cut])
            for i, (source, target) in enumerate(pairs)
        ]

    for cut in range(len(cuts)):
        for copy in fetch(cut):
            copy.start()
    for i, (source, target) in enumerate(((q_in, q_ref), (r_in, r_ref))):
        target[:, : HEAD * LANES] = source[...]
    if early:
        columns = pl.ds((first + count) * LANES, HEAD * LANES)
        pairs = (
            (gated_hbm.at[pl.ds(0, HEAD)], gated_next),
            (q_hbm.at[:, columns], q_next),
            (res_hbm.at[:, columns], r_next),
        )
        ahead_of_time = [
            pltpu.make_async_copy(source, target, next_sems.at[i]) for i, (source, target) in enumerate(pairs)
        ]
        for copy in ahead_of_time:
            copy.start()
        rank_factors(info_ref, rows, poles, rate_ref, factor_ref)
    else:
        gated_ref[:HEAD] = gated_in[...]
    span = rows // CHUNKS
    chunk = lax.broadcasted_iota(jnp.int32, (CHUNKS, LANES), 0)
    flags = [
        jnp.max(info_ref[FLAGS.start + block : FLAGS.start + block + 1, :]) > 0.0
        for block in range(span // STEPS)
    ]

    made = (near_ref, query_ref, local_ref)

    def store(here, targets, low):
        return [
            pltpu.make_async_copy(source.at[here], target.at[here - low], far_sems.at[i, here])
            for i, (source, target) in enumerate(zip(made, targets))
        ]

    @pl.loop(0, count)
    def _(here):
        own = lanes_at(here)
        lanes = lanes_at(here + first)
        far = info_ref[FAR, :]
        joined = info_ref[JOINED, :]

        for cut, (low, _) in enumerate(cuts):

            @pl.when(here == low)
            def _():
                for copy in fetch(cut):
                    copy.wait()

        qx[5:7, :] = rim_ref[:, lanes].astype(F32)
        lay_out(q_ref, own, qx, span, 8)
        lay_out(r_ref, own, rx, span, 0)
        decay_ref[...] = jnp.exp(-rate_ref[:, lanes])
        taps = [spread(taps_ref[j : j + 1, lanes]) for j in range(3)]
        skip = spread(skip_ref[:, lanes])
        decay = [spread(decay_ref[m : m + 1, :]) for m in range(poles)]
        gain = [spread(gain_ref[m : m + 1, lanes]) for m in range(poles)]
        carry = [
            qx[pl.ds(6, CHUNKS, stride=span + 1), :],
            qx[pl.ds(5, CHUNKS, stride=span + 1), :] * far,
        ] + [jnp.zeros((CHUNKS, LANES), F32)] * poles

        def run(block, masked, carry):
            carry = list(carry)
            for step in range(STEPS):
                place = block * STEPS + step
                if masked:
                    keep = jnp.ones((CHUNKS, LANES), F32)
                    for i in range(SEGMENTS):
                        low = INSIDE.start + i * CHUNKS
                        keep = jnp.where(info_ref[low : low + CHUNKS, :] == float(place), 0.0, keep)
                    carry = [held * keep for held in carry]
                query = qx[pl.ds(8 + place, CHUNKS, stride=span + 1), :]
                query_short = taps[0] * query + taps[1] * carry[0] + taps[2] * carry[1]
                gated = gated_ref[here, pl.ds(place, CHUNKS, stride=span + 1), :]
                if place < 2:
                    edge = spread(edge_ref[here + first, place : place + 1, :])
                    gated = jnp.where(chunk == 0, edge, gated)
                states = [decay[m] * carry[2 + m] + gated for m in range(poles)]
                total = skip * gated
                for m in range(poles):
                    total = total + gain[m] * states[m]
                query_ref[here, chunk_of(place), :] = query_short
                near_ref[here, chunk_of(place), :] = (
                    rx[pl.ds(place, CHUNKS, stride=span + 1), :] + query_short * total
                )
                carry = [query, carry[0]] + states
            return tuple(carry)

        carry = walk(span, flags, run, tuple(carry))
        for m in range(poles):
            reach = jnp.exp(-float(span) * spread(rate_ref[m : m + 1, lanes])) * joined
            state = carry[2 + m]
            for hop in (1, 2, 4):
                state = state + reach * pltpu.roll(state, hop, 0)
                if hop < 4:
                    reach = reach * pltpu.roll(reach, hop, 0)
            local_ref[here, m * CHUNKS : (m + 1) * CHUNKS, :] = jnp.where(
                chunk > 0, pltpu.roll(state, 1, 0), 0.0
            )
        if early:
            for copy in store(here, outs, 0):
                copy.start()
        else:

            @pl.when(here < READY)
            def _():
                for source, target in zip(made, heads):
                    target[here] = source[here]

            @pl.when(here >= READY)
            def _():
                for copy in store(here, tails, READY):
                    copy.start()

    if early:
        for copy in ahead_of_time:
            copy.wait()
    for here in range(0 if early else READY, count):
        for copy in store(here, outs, 0) if early else store(here, tails, READY):
            copy.wait()


def stream_kernel(rows, poles, info_ref, rate_ref, gain_ref, incoming_ref, near_hbm, query_hbm, local_hbm, near_head, query_head, local_head, near_rest, query_rest, local_rest, out_hbm, stream_ref, power_ref, near_a, query_a, local_a, near_b, query_b, local_b, sx, px, decay_ref, sems, far_sems, rest_sems):
    span = rows // CHUNKS
    chunk = lax.broadcasted_iota(jnp.int32, (CHUNKS, LANES), 0)
    px[...] = jnp.zeros_like(px)
    inner = GROUP // LANES
    early = near_a.shape[0]

    def fetch(group):
        here = pl.ds(group * inner, inner)
        pairs = ((near_hbm, near_a), (query_hbm, query_a), (local_hbm, local_a))
        return [
            pltpu.make_async_copy(source.at[here], target.at[here], far_sems.at[i, group])
            for i, (source, target) in enumerate(pairs)
        ]

    pairs = ((near_rest, near_b), (query_rest, query_b), (local_rest, local_b))
    rest = [pltpu.make_async_copy(source, target, rest_sems.at[i]) for i, (source, target) in enumerate(pairs)]
    for group in range(early // inner):
        for copy in fetch(group):
            copy.start()
    for copy in rest:
        copy.start()
    before = (chunk * span).astype(F32)

    def copy_out(group):
        lanes = pl.ds(pl.multiple_of(group * GROUP, GROUP), GROUP)
        return pltpu.make_async_copy(stream_ref.at[:, lanes], out_hbm.at[:, lanes], sems.at[group])

    def one_part(part, near_ref, query_ref, local_ref, place_of):
        lanes = lanes_at(part)
        decay_ref[...] = jnp.exp(-rate_ref[:, lanes])
        decay = [spread(decay_ref[m : m + 1, :]) for m in range(poles)]
        reached = info_ref[REACHED, :]
        ahead = info_ref[AHEAD, :]
        carry = []
        for m in range(poles):
            entering = reached * jnp.exp(-before * spread(rate_ref[m : m + 1, lanes]))
            entering = entering * spread(incoming_ref[part, m : m + 1, :])
            entering = entering + local_ref[place_of, m * CHUNKS : (m + 1) * CHUNKS, :]
            carry.append(spread(gain_ref[m : m + 1, lanes]) * entering)
        for place in range(span):
            carry = [decay[m] * carry[m] for m in range(poles)]
            terms = list(carry)
            while len(terms) > 1:
                terms = [
                    terms[i] + terms[i + 1] if i + 1 < len(terms) else terms[i]
                    for i in range(0, len(terms), 2)
                ]
            carried = jnp.where(ahead > float(place), terms[0], 0.0)
            here = chunk_of(place)
            sx[pl.ds(place, CHUNKS, stride=span + 1), :] = (
                near_ref[place_of, here, :] + query_ref[place_of, here, :] * carried
            )
        for piece in range(CHUNKS):
            low = piece * (span + 1)
            stream = sx[low : low + span, :]
            native = slice(piece * span, (piece + 1) * span)
            stream_ref[native, lanes] = stream
            px[native, :] += stream * stream

    groups = stream_ref.shape[1] // GROUP
    sides = (
        (early, near_head, query_head, local_head),
        (0, near_a, query_a, local_a),
        (early + READY, near_b, query_b, local_b),
    )
    for first, near_ref, query_ref, local_ref in sides:

        @pl.loop(0, near_ref.shape[0] // inner)
        def _(group):
            if near_ref is near_a:
                for copy in fetch(group):
                    copy.wait()
            if near_ref is near_b:
                for copy in rest:
                    copy.wait()

            @pl.loop(group * inner, (group + 1) * inner)
            def _(part):
                one_part(part + first, near_ref, query_ref, local_ref, part)

            if near_ref is not near_b:
                copy_out(group + first // inner).start()

    for piece in range(rows // LANES):
        turned = px[piece * LANES : (piece + 1) * LANES, :].T
        power_ref[piece : piece + 1, :] = jnp.sum(turned, axis=0, keepdims=True)
    for group in range((early + READY) // inner):
        copy_out(group).wait()


def norm_kernel(width, left, power_ref, gain_ref, stream_ref, stream_in, out_hbm, stream_out, scale_ref, buffer, sems, left_sem):
    columns = pl.ds(left, stream_ref.shape[1] - left)
    rest = pltpu.make_async_copy(stream_ref.at[:, columns], stream_out.at[:, columns], left_sem.at[0])
    rest.start()
    scale = lax.rsqrt(jnp.sum(power_ref[...], axis=0) / width + 1e-06)
    for piece in range(scale.shape[0]):
        wide = jnp.broadcast_to(scale[piece : piece + 1, :], (LANES, LANES))
        scale_ref[piece * LANES : (piece + 1) * LANES, :] = wide.T
    rows = stream_ref.shape[0]
    count = sems.shape[0]
    tall = rows // count

    def copy_out(group):
        here = pl.ds(pl.multiple_of(group * tall, tall), tall)
        return pltpu.make_async_copy(buffer.at[here, :], out_hbm.at[here, :], sems.at[group])

    @pl.loop(0, count)
    def _(group):
        here = pl.ds(pl.multiple_of(group * tall, tall), tall)
        factor = scale_ref[here, :]
        for part in range(stream_ref.shape[1] // LANES):
            lanes = slice(part * LANES, (part + 1) * LANES)
            buffer[here, lanes] = stream_ref[here, lanes] * factor * gain_ref[:, lanes]
        copy_out(group).start()

    for group in range(count):
        copy_out(group).wait()
    rest.wait()


def shifted(block, axis, distance):
    count = lax.axis_size(axis)
    return lax.ppermute(block, axis, [(i, (i + distance) % count) for i in range(count)])


def on_device(query_proj, key_proj, value_proj, short_filter, decay_rate, residue, skip_gain, norm_gain, residual, lengths):
    rows, width = query_proj.shape
    poles = decay_rate.shape[0]
    ranks = lax.axis_size("ctx")
    parts = width // LANES
    groups = width // GROUP
    near_by = pl.BlockSpec(memory_space=pltpu.VMEM)
    outside = pl.BlockSpec(memory_space=pltpu.HBM)
    limit = pltpu.CompilerParams(vmem_limit_bytes=12 * 1024 * 1024)
    shape = lambda *dims: jax.ShapeDtypeStruct(dims, F32)
    kept_near = lambda *dims: pltpu.VMEM(dims, F32)
    far_off = lambda array: pltpu.with_memory_space_constraint(array, pltpu.HBM)
    close_by = lambda array: pltpu.with_memory_space_constraint(array, pltpu.VMEM)
    query_proj, key_proj, value_proj, residual, short_filter, lengths = map(
        far_off, (query_proj, key_proj, value_proj, residual, short_filter, lengths)
    )

    rims = pl.pallas_call(
        rim_kernel,
        in_specs=[outside] * 3,
        out_specs=near_by,
        out_shape=pltpu.VMEM((3, 2, width), BF16),
        scratch_shapes=[pltpu.VMEM((3, 16, width), BF16), pltpu.SemaphoreType.DMA((3,))],
        name="rims",
    )(query_proj, key_proj, value_proj)
    rims = shifted(rims, "ctx", 1)
    pole_gain = residue * jnp.sqrt(-jnp.expm1(-2.0 * decay_rate))
    skip = skip_gain.reshape(1, width)

    early = FIRST_SHARE * (GROUP // LANES)
    late = parts - early
    pitch = rows + CHUNKS
    held = parts * poles // ranks
    k_here, v_here, q_a, r_a, taps_here, info = pl.pallas_call(
        functools.partial(fetch_kernel, rows),
        in_specs=[outside] * 6,
        out_specs=[near_by] * 6,
        out_shape=[
            pltpu.VMEM((rows, width), BF16),
            pltpu.VMEM((rows, width), BF16),
            pltpu.VMEM((rows, HEAD * LANES), BF16),
            pltpu.VMEM((rows, HEAD * LANES), BF16),
            kept_near(3, 3, width),
            kept_near(SECTIONS, LANES),
        ],
        scratch_shapes=[pltpu.SMEM(lengths.shape, jnp.int32), pltpu.SemaphoreType.DMA((6,))],
        compiler_params=limit,
        cost_estimate=pl.CostEstimate(flops=1000000, bytes_accessed=5000000, transcendentals=0),
        name="fetch",
    )(lengths, key_proj, value_proj, query_proj, residual, short_filter)
    info, k_here, v_here, taps_here = map(close_by, (info, k_here, v_here, taps_here))
    gated_a, gated_b, partial = pl.pallas_call(
        functools.partial(end_kernel, rows, poles),
        in_specs=[near_by] * 5,
        out_specs=[near_by, outside, near_by],
        out_shape=[
            kept_near(early, pitch, LANES),
            pltpu.HBM((late, pitch, LANES), F32),
            kept_near(parts, poles, LANES),
        ],
        scratch_shapes=[
            pltpu.VMEM((late, pitch, LANES), F32),
            pltpu.VMEM((rows + 8, LANES), F32),
            pltpu.VMEM((rows + 8, LANES), F32),
            pltpu.VMEM((rows, LANES), F32),
            pltpu.VMEM((poles, LANES), F32),
            pltpu.SMEM((2, 8), jnp.int32),
            pltpu.SemaphoreType.DMA((late,)),
        ],
        compiler_params=limit,
        cost_estimate=pl.CostEstimate(flops=4000000, bytes_accessed=8000000, transcendentals=0),
        name="end_state",
    )(info, k_here, v_here, taps_here, decay_rate)
    end, edges, query_rim, query_taps = pl.pallas_call(
        functools.partial(edge_kernel, rows, poles),
        in_specs=[near_by] * 7,
        out_specs=[outside, near_by, near_by, near_by],
        out_shape=[
            pltpu.HBM((parts, poles, LANES), F32),
            kept_near(parts, CHUNKS, LANES),
            pltpu.VMEM((2, width), BF16),
            kept_near(3, width),
        ],
        scratch_shapes=[pltpu.VMEM((parts, poles, LANES), F32), pltpu.SemaphoreType.DMA((groups,))],
        compiler_params=limit,
        name="edges",
    )(info, k_here, v_here, rims, taps_here, decay_rate, close_by(partial))
    edges = close_by(edges)
    query_rim, query_taps = map(close_by, (query_rim, query_taps))

    pieces = lax.all_to_all(end.reshape(ranks, held, LANES), "ctx", 0, 0, tiled=True)

    def near_side(first, count, gated, q_part, r_part, early):
        block = (count, rows, LANES)
        states = (count, poles * CHUNKS, LANES)
        given = [info, query_rim, query_taps, decay_rate, pole_gain, skip, edges, *map(close_by, (gated, q_part, r_part))]
        fetched = [query_proj, residual, far_off(gated_b)]
        scratch = [
            pltpu.VMEM((rows, count * LANES), BF16),
            pltpu.VMEM((rows, count * LANES), BF16),
            pltpu.VMEM((rows + 16, LANES), F32),
            pltpu.VMEM((rows + 16, LANES), F32),
            pltpu.VMEM((poles, LANES), F32),
            pltpu.SemaphoreType.DMA((3, 2)),
            pltpu.SemaphoreType.DMA((3, count)),
        ]
        if early:
            out_specs = [outside] * 3 + [near_by] * 4
            out_shape = [pltpu.HBM(dims, F32) for dims in (block, block, states)] + [
                kept_near(ranks, held, LANES),
                kept_near(HEAD, pitch, LANES),
                pltpu.VMEM((rows, HEAD * LANES), BF16),
                pltpu.VMEM((rows, HEAD * LANES), BF16),
            ]
            scratch = [pltpu.VMEM(dims, F32) for dims in (block, block, states)] + scratch
            scratch += [pltpu.SemaphoreType.DMA((3,))]
        else:
            out_specs = [near_by] * 3 + [outside] * 3
            out_shape = [kept_near(READY, *dims[1:]) for dims in (block, block, states)]
            out_shape += [pltpu.HBM((count - READY, *dims[1:]), F32) for dims in (block, block, states)]
            scratch = [pltpu.VMEM(dims, F32) for dims in ((count, pitch, LANES), block, block, states)] + scratch
        return pl.pallas_call(
            functools.partial(near_kernel, rows, poles, first, early),
            in_specs=[near_by] * len(given) + [outside] * len(fetched),
            out_specs=out_specs,
            out_shape=out_shape,
            scratch_shapes=scratch,
            compiler_params=limit,
            cost_estimate=pl.CostEstimate(flops=4000000, bytes_accessed=8000000, transcendentals=0),
            name="near",
        )(*given, *fetched)

    near_a, query_a, local_a, factors, gated_head, q_b, r_b = near_side(0, early, gated_a, q_a, r_a, True)
    near_b = near_side(early, late, gated_head, q_b, r_b, False)
    scanned = pl.pallas_call(
        scan_kernel,
        in_specs=[near_by, near_by],
        out_specs=outside,
        out_shape=pltpu.HBM((ranks, held, LANES), F32),
        scratch_shapes=[pltpu.VMEM((ranks, held, LANES), F32), pltpu.SemaphoreType.DMA((2,))],
        compiler_params=limit,
        name="rank_scan",
    )(close_by(factors), pieces)
    incoming = lax.all_to_all(scanned, "ctx", 0, 0, tiled=True).reshape(parts, poles, LANES)

    stream, kept, power = pl.pallas_call(
        functools.partial(stream_kernel, rows, poles),
        in_specs=[near_by] * 4 + [outside] * 3 + [near_by] * 3 + [outside] * 3,
        out_specs=[outside, near_by, near_by],
        out_shape=[pltpu.HBM((rows, width), F32), kept_near(rows, width), kept_near(rows // LANES, LANES)],
        scratch_shapes=[
            pltpu.VMEM((early, rows, LANES), F32),
            pltpu.VMEM((early, rows, LANES), F32),
            pltpu.VMEM((early, poles * CHUNKS, LANES), F32),
            pltpu.VMEM((late - READY, rows, LANES), F32),
            pltpu.VMEM((late - READY, rows, LANES), F32),
            pltpu.VMEM((late - READY, poles * CHUNKS, LANES), F32),
            pltpu.VMEM((rows + 8, LANES), F32),
            pltpu.VMEM((rows, LANES), F32),
            pltpu.VMEM((poles, LANES), F32),
            pltpu.SemaphoreType.DMA((groups,)),
            pltpu.SemaphoreType.DMA((3, early // (GROUP // LANES))),
            pltpu.SemaphoreType.DMA((3,)),
        ],
        compiler_params=limit,
        name="stream",
    )(
        info,
        decay_rate,
        pole_gain,
        incoming,
        *map(far_off, (near_a, query_a, local_a)),
        *map(close_by, near_b[:3]),
        *map(far_off, near_b[3:]),
    )
    shares = lax.axis_size("ch")
    near_first = sorted(range(1, shares), key=lambda hop: min(hop, shares - hop))
    powers = jnp.stack([power] + [shifted(power, "ch", hop) for hop in near_first])
    normed, stream = pl.pallas_call(
        functools.partial(norm_kernel, float(width * shares), (early + READY) * LANES),
        in_specs=[near_by, near_by, near_by, outside],
        out_specs=[outside, outside],
        out_shape=[pltpu.HBM((rows, width), F32)] * 2,
        input_output_aliases={3: 1},
        scratch_shapes=[
            pltpu.VMEM((rows, LANES), F32),
            pltpu.VMEM((rows, width), F32),
            pltpu.SemaphoreType.DMA((8,)),
            pltpu.SemaphoreType.DMA((1,)),
        ],
        compiler_params=limit,
        name="norm",
    )(powers, norm_gain.reshape(1, width), close_by(kept), far_off(stream))
    return (stream, normed)


def solution(mesh):
    placed = (
        P("ctx", "ch"),
        P("ctx", "ch"),
        P("ctx", "ch"),
        P(None, None, "ch"),
        P(None, "ch"),
        P(None, "ch"),
        P("ch"),
        P("ch"),
        P("ctx", "ch"),
        P(),
    )
    return jax.shard_map(
        on_device,
        mesh=mesh,
        in_specs=placed,
        out_specs=(P("ctx", "ch"), P("ctx", "ch")),
        check_vma=False,
    )
```
